32 devices in a mesh: user: 8 (over y, x, core), item: 4 (over z).
Axes of the slice: x: 2, y: 2, z: 4, core: 2. Of those that a mesh axis runs over, the one named last changes fastest.
Arguments:
- user_pred: bfloat16 [8192, 128], P('user'), may hold values from -1.75 to 1.75
- user_imp: bfloat16 [8192, 128], P('user'), may hold values from -1.75 to 1.75
- item_pred: bfloat16 [1024, 128], P('item'), may hold values from -1.75 to 1.75
- item_imp: bfloat16 [1024, 128], P('item'), may hold values from -1.75 to 1.75
- uno_user: int32 [8, 4, 64], P('user', 'item'), may hold values from 0 to 7
- uno_item: int32 [8, 4, 64], P('user', 'item'), may hold values from 0 to 1
- obs_user: int32 [8, 4, 16], P('user', 'item'), may hold values from 0 to 7
- obs_item: int32 [8, 4, 16], P('user', 'item'), may hold values from 0 to 1
- obs_count: int32 [8, 4, 4], P('user', 'item'), may hold values from 0 to 4
- obs_label: int32 [8, 4, 16, 128, 128], P('user', 'item'), may hold values from 0 to 2
- obs_prop: bfloat16 [8, 4, 16, 128, 128], P('user', 'item'), may hold values from 0.099609375 to 1
Outputs:
- user_pred_grad: float32 [8192, 128], P(('user', 'item'))
- user_imp_grad: float32 [8192, 128], P(('user', 'item'))
- item_pred_grad: float32 [1024, 128], P(('item', 'user'))
- item_imp_grad: float32 [1024, 128], P(('item', 'user'))
The draws below stay inside these ranges and needn't reach their ends.
Inputs may be any that keep to these rules, and one draw needn't show every extreme that they name: `uno_item`: each device's unobserved slots come in equal groups, one group for each item shard in order. Each device's observed slots come in equal groups of 16 / number of item indices, one group for each item shard in order; only the first obs_count slots of a group hold tiles.
All inputs are finite; a program needn't handle non-finite values.
Results may differ from the reference program's by a relative error of at most 0.0027.
Values may be sent and summed in bfloat16 or wider, within the bound.
No kernel may reach another device: no remote copies, remote signals or barrier semaphores. Data moves between devices by JAX's collectives and lax.ppermute only.
A program may use at most 64 MiB of HBM per device.

```python
import math
import jax
import jax.numpy as jnp
from jax import lax

R = 128
TILE = 128
SH = 1024
ISH = 256
UNO_DEV = 64
OBS_DEV = 16
USERS = 8192
ITEMS = 1024
N_USER = 8
N_ITEM = 4


def touch_ends(entries, rng, low, high):
    place = [jax.random.randint(jax.random.fold_in(rng, axis), (), 0, length) for axis, length in enumerate(entries.shape)]
    main_axis = entries.shape.index(max(entries.shape))
    next_to = place[:main_axis] + [(place[main_axis] + 1) % entries.shape[main_axis]] + place[main_axis + 1:]
    return entries.at[tuple(place)].set(low).at[tuple(next_to)].set(high)


def block_levels(stream_key, dims, shards, low, largest):
    gain = 1.0
    for axis_at, parts in shards:
        steps = jax.random.uniform(jax.random.fold_in(jax.random.fold_in(stream_key, 6), axis_at), (parts,), jnp.float32, low / len(shards), largest / len(shards))
        gain = gain * jnp.repeat(jnp.exp(steps), dims[axis_at] // parts).reshape((-1,) + (1,) * (len(dims) - 1 - axis_at))
    return gain


def centred(own_key, extent, width, bound, pieces=(), held_as=jnp.bfloat16):
    factor_of = block_levels(own_key, extent, pieces, -0.22, 0.18) if pieces else 1.0
    array = jax.random.normal(own_key, extent, jnp.float32) * width * factor_of
    return jnp.minimum(jnp.maximum(array, -bound), bound).astype(held_as)


def setup_inputs(seed: int = 0) -> dict:
    streams_of = jax.random.split(jax.random.key(seed), 12)
    return {
        "user_pred": centred(streams_of[0], (USERS, R), 0.3, 1.75, ((0, 8),)),
        "user_imp": centred(streams_of[1], (USERS, R), 0.3, 1.75, ((0, 8),)),
        "item_pred": centred(streams_of[2], (ITEMS, R), 0.3, 1.75, ((0, 4),)),
        "item_imp": centred(streams_of[3], (ITEMS, R), 0.3, 1.75, ((0, 4),)),
        "uno_user": touch_ends(jax.random.randint(streams_of[4], (N_USER, N_ITEM, UNO_DEV), 0, SH // TILE), jax.random.fold_in(streams_of[4], 1), 0, (SH // TILE) - 1).astype(jnp.int32),
        "uno_item": touch_ends(jax.random.randint(streams_of[5], (N_USER, N_ITEM, UNO_DEV), 0, ISH // TILE), jax.random.fold_in(streams_of[5], 1), 0, (ISH // TILE) - 1).astype(jnp.int32),
        "obs_user": touch_ends(jax.random.randint(streams_of[6], (N_USER, N_ITEM, OBS_DEV), 0, SH // TILE), jax.random.fold_in(streams_of[6], 1), 0, (SH // TILE) - 1).astype(jnp.int32),
        "obs_item": touch_ends(jax.random.randint(streams_of[7], (N_USER, N_ITEM, OBS_DEV), 0, ISH // TILE), jax.random.fold_in(streams_of[7], 1), 0, (ISH // TILE) - 1).astype(jnp.int32),
        "obs_count": touch_ends(jax.random.randint(streams_of[8], (N_USER, N_ITEM, N_ITEM), 0, OBS_DEV // N_ITEM + 1), jax.random.fold_in(streams_of[8], 1), 0, (OBS_DEV // N_ITEM + 1) - 1).astype(jnp.int32),
        "obs_label": touch_ends(jax.random.randint(streams_of[9], (N_USER, N_ITEM, OBS_DEV, TILE, TILE), 0, 3), jax.random.fold_in(streams_of[9], 1), 0, 2).astype(jnp.int32),
        "obs_prop": jnp.clip(jnp.exp(math.log(1.0) - 2.306499 * jax.random.uniform(streams_of[10], (N_USER, N_ITEM, OBS_DEV, TILE, TILE), jnp.float32) ** block_levels(streams_of[10], (N_USER, N_ITEM, OBS_DEV, TILE, TILE), ((0, 8), (1, 4)), -0.2, 0.2)), 0.099609375, 1.0).astype(jnp.bfloat16),
    }


loss_weight = 0.015625


def batched(form, first, second):
    return jnp.einsum(form, first.astype(jnp.float32), second.astype(jnp.float32), precision=lax.Precision.HIGHEST)


def reference(user_pred, user_imp, item_pred, item_imp, uno_user, uno_item, obs_user, obs_item, obs_count, obs_label, obs_prop):
    user_blocks = SH // TILE
    item_blocks = ISH // TILE
    all_blocks = ITEMS // TILE
    uno_slots = UNO_DEV // N_ITEM
    obs_slots = OBS_DEV // N_ITEM
    users_both = jnp.stack([user_pred, user_imp]).reshape(2, N_USER, user_blocks, TILE, R)
    items_both = jnp.stack([item_pred, item_imp]).reshape(2, all_blocks, TILE, R)
    uno_shard = (jnp.arange(UNO_DEV) // uno_slots).astype(jnp.int32)
    obs_shard = (jnp.arange(OBS_DEV) // obs_slots).astype(jnp.int32)
    obs_place = (jnp.arange(OBS_DEV) % obs_slots).astype(jnp.int32)

    def device(carry, index):
        user_acc, item_acc = carry
        row_index = index // N_ITEM
        col_index = index % N_ITEM
        own_pred = users_both[0, row_index]
        own_imp = users_both[1, row_index]
        user_ids = uno_user[row_index, col_index]
        item_ids = uno_shard * item_blocks + uno_item[row_index, col_index]
        user_tiles = own_pred[user_ids]
        item_tiles = items_both[0][item_ids]
        logits = batched("tar,tbr->tab", user_tiles, item_tiles)
        imputed = batched("tar,tbr->tab", own_imp[user_ids], items_both[1][item_ids])
        grads = ((jax.nn.sigmoid(logits) - jax.nn.sigmoid(imputed)) * loss_weight).astype(jnp.bfloat16)
        user_part = jax.ops.segment_sum(batched("tab,tbr->tar", grads, item_tiles), user_ids, num_segments=user_blocks)
        item_part = jax.ops.segment_sum(batched("tab,tar->tbr", grads, user_tiles), item_ids, num_segments=all_blocks)

        obs_users = obs_user[row_index, col_index]
        obs_items = obs_shard * item_blocks + obs_item[row_index, col_index]
        ou_tiles = own_pred[obs_users]
        ox_tiles = own_imp[obs_users]
        ov_tiles = items_both[0][obs_items]
        oy_tiles = items_both[1][obs_items]
        ologits = batched("tar,tbr->tab", ou_tiles, ov_tiles)
        oimputed = batched("tar,tbr->tab", ox_tiles, oy_tiles)
        predicted = jax.nn.sigmoid(ologits)
        imputes = jax.nn.sigmoid(oimputed)
        counts = obs_count[row_index, col_index][obs_shard]
        valid = (obs_place < counts).astype(jnp.float32)[:, None, None]
        labels = obs_label[row_index, col_index]
        seen = (labels > 0).astype(jnp.float32)
        clicks = (labels == 2).astype(jnp.float32)
        weight = valid * seen / obs_prop[row_index, col_index].astype(jnp.float32)
        ograds = ((valid * (predicted - imputes) + weight * (imputes - clicks)) * loss_weight).astype(jnp.bfloat16)
        ohgrads = (2.0 * weight * (imputes - clicks) * ologits * ologits * imputes * (1.0 - imputes) * loss_weight).astype(jnp.bfloat16)
        user_part = user_part + jax.ops.segment_sum(batched("tab,tbr->tar", ograds, ov_tiles), obs_users, num_segments=user_blocks)
        user_imp_part = jax.ops.segment_sum(batched("tab,tbr->tar", ohgrads, oy_tiles), obs_users, num_segments=user_blocks)
        item_part = item_part + jax.ops.segment_sum(batched("tab,tar->tbr", ograds, ou_tiles), obs_items, num_segments=all_blocks)
        item_imp_part = jax.ops.segment_sum(batched("tab,tar->tbr", ohgrads, ox_tiles), obs_items, num_segments=all_blocks)
        user_acc = user_acc.at[:, row_index].add(jnp.stack([user_part, user_imp_part]))
        item_acc = item_acc + jnp.stack([item_part, item_imp_part])
        return (user_acc, item_acc), None

    start = (jnp.zeros((2, N_USER, user_blocks, TILE, R), jnp.float32), jnp.zeros((2, all_blocks, TILE, R), jnp.float32))
    (user_acc, item_acc), unused = lax.scan(device, start, jnp.arange(N_USER * N_ITEM, dtype=jnp.int32))
    user_acc = user_acc.reshape(2, USERS, R)
    item_acc = item_acc.reshape(2, ITEMS, R)
    return (user_acc[0], user_acc[1], item_acc[0], item_acc[1])
```

```python
import jax
import jax.numpy as jnp
from jax import lax
from jax.experimental import pallas as pl
from jax.experimental.pallas import tpu as pltpu
from jax.sharding import PartitionSpec as P

loss_weight = 0.015625
cores = 2
vmem_bytes = 48 * 1024 * 1024

VM = pl.BlockSpec(memory_space=pltpu.VMEM)
SM = pl.BlockSpec(memory_space=pltpu.SMEM)


def dot(first, second, dims):
    return lax.dot_general(first, second, (dims, ((), ())), preferred_element_type=jnp.float32)


def rows_by_cols(first, second):
    return dot(first, second, ((1,), (1,)))


def plain(first, second):
    return dot(first, second, ((1,), (0,)))


def over_rows(first, second):
    return dot(first, second, ((0,), (0,)))


def call(body, name, out_shapes, specs, args, cost, scratch=()):
    return pl.pallas_call(
        body,
        out_shape=out_shapes,
        in_specs=specs,
        out_specs=tuple(VM for _ in out_shapes),
        scratch_shapes=list(scratch),
        compiler_params=pltpu.CompilerParams(vmem_limit_bytes=vmem_bytes),
        cost_estimate=pl.CostEstimate(flops=cost[0], bytes_accessed=cost[1], transcendentals=cost[2]),
        name=name,
    )(*args)


def shape(dims, kind):
    return jax.ShapeDtypeStruct(dims, kind)


def shards(
    user_pred,
    user_imp,
    item_pred,
    item_imp,
    uno_user,
    uno_item,
    obs_user,
    obs_item,
    obs_count,
    obs_label,
    obs_prop,
):
    item_ways = lax.axis_size("item")
    user_ways = lax.axis_size("user")
    chips = user_ways // cores
    tile = obs_label.shape[-1]
    rank = user_pred.shape[1]
    user_rows = user_pred.shape[0]
    shard_rows = item_pred.shape[0]
    user_blocks = user_rows // tile
    item_blocks = shard_rows // tile
    pairs = user_blocks * item_blocks
    half = shard_rows // cores
    share = user_rows // item_ways
    item_share = shard_rows // user_ways
    uno_slots = uno_user.shape[-1] // item_ways
    obs_all = obs_user.shape[-1]
    obs_slots = obs_all // item_ways
    peers = item_ways - 1
    f32 = jnp.float32
    bf16 = jnp.bfloat16

    place = jnp.stack([lax.axis_index("item"), lax.axis_index("user")]).astype(jnp.int32)
    uno_user = uno_user.reshape(-1)
    uno_item = uno_item.reshape(-1)
    obs_user = obs_user.reshape(-1)
    obs_item = obs_item.reshape(-1)
    obs_count = obs_count.reshape(-1)
    labels = obs_label.reshape(obs_all, tile, tile)
    propens = obs_prop.reshape(obs_all, tile, tile)

    def item_peer(x, k):
        return lax.ppermute(x, "item", [(i, i ^ k) for i in range(item_ways)])

    def core_peer(x):
        return lax.ppermute(x, "user", [(i, i ^ 1) for i in range(user_ways)])

    def chip_peer(x, k):
        return lax.ppermute(x, "user", [(i, i ^ (cores * k)) for i in range(user_ways)])

    def pack(place_ref, uu_ref, ui_ref, vp_ref, vi_ref, *outs):
        pos = place_ref[0]
        core = lax.rem(place_ref[1], cores)
        start = pl.multiple_of(core * half, half)
        row = lax.broadcasted_iota(jnp.int32, (pairs, rank), 0)
        for k in range(item_ways):
            group = lax.bitwise_xor(pos, k)
            count = jnp.zeros((pairs, rank), f32)
            for s in range(uno_slots):
                at = group * uno_slots + s
                pair = uu_ref[at] * item_blocks + ui_ref[at]
                count = count + jnp.where(row == pair, 1.0, 0.0)
            if k == 0:
                outs[peers][...] = count
            else:
                out = outs[k - 1]
                out[0:half] = vp_ref[pl.ds(start, half)]
                out[half : 2 * half] = vi_ref[pl.ds(start, half)]
                out[2 * half :] = count.astype(bf16)

    packed = call(
        pack,
        "pack",
        tuple(shape((2 * half + pairs, rank), bf16) for _ in range(peers)) + (shape((pairs, rank), f32),),
        [SM, SM, SM, VM, VM],
        (place, uno_user, uno_item, item_pred, item_imp),
        (0, 400000, 0),
    )
    own_count = packed[peers]
    received = [item_peer(packed[k], k + 1) for k in range(peers)]
    swapped = [core_peer(x) for x in received]

    def observed(logits, imputed, weight, used):
        p = jax.nn.sigmoid(logits)
        q = jax.nn.sigmoid(imputed)
        miss = q - jnp.where(weight < 0, 1.0, 0.0)
        term = jnp.abs(weight) * miss
        g = (((p - q) + term) * (used * loss_weight)).astype(bf16)
        h = (2.0 * term * logits * logits * q * (1.0 - q) * (used * loss_weight)).astype(bf16)
        return g, h

    def local(
        place_ref, ou_ref, oi_ref, oc_ref, up_ref, ux_ref, vp_ref, vi_ref, lab_ref, prop_ref,
        utile_ref, itile_ref, uacc_ref, iacc_ref, w_ref,
    ):
        pos = place_ref[0]
        for t in range(obs_all):
            state = lab_ref[t]
            inverse = 1.0 / prop_ref[t].astype(f32)
            w_ref[t] = jnp.where(state == 0, 0.0, jnp.where(state == 2, -inverse, inverse))
        for u in range(user_blocks):
            urows = pl.ds(u * tile, tile)
            for b in range(item_blocks):
                irows = pl.ds(b * tile, tile)
                logits = rows_by_cols(up_ref[urows], vp_ref[irows])
                imputed = rows_by_cols(ux_ref[urows], vi_ref[irows])
                g = ((jax.nn.sigmoid(logits) - jax.nn.sigmoid(imputed)) * loss_weight).astype(bf16)
                utile_ref[u * item_blocks + b] = plain(g, vp_ref[irows])
                itile_ref[u * item_blocks + b] = over_rows(g, up_ref[urows])
        uacc_ref[...] = jnp.zeros_like(uacc_ref)
        iacc_ref[...] = jnp.zeros_like(iacc_ref)
        for s in range(obs_slots):
            at = pos * obs_slots + s
            urows = pl.ds(pl.multiple_of(ou_ref[at] * tile, tile), tile)
            irows = pl.ds(pl.multiple_of(oi_ref[at] * tile, tile), tile)
            used = jnp.where(s < oc_ref[pos], 1.0, 0.0)
            logits = rows_by_cols(up_ref[urows], vp_ref[irows])
            imputed = rows_by_cols(ux_ref[urows], vi_ref[irows])
            g, h = observed(logits, imputed, w_ref[at], used)
            uacc_ref[0, urows] += plain(g, vp_ref[irows])
            uacc_ref[1, urows] += plain(h, vi_ref[irows])
            iacc_ref[0, irows] += over_rows(g, up_ref[urows])
            iacc_ref[1, irows] += over_rows(h, ux_ref[urows])

    utile, itile, uacc, iacc, weights = call(
        local,
        "local_tiles",
        (
            shape((pairs, tile, rank), f32),
            shape((pairs, tile, rank), f32),
            shape((2, user_rows, rank), f32),
            shape((2, shard_rows, rank), f32),
            shape((obs_all, tile, tile), f32),
        ),
        [SM, SM, SM, SM, VM, VM, VM, VM, VM, VM],
        (place, obs_user, obs_item, obs_count, user_pred, user_imp, item_pred, item_imp, labels, propens),
        (4 * pairs * 2 * tile**3, 8000000, 2 * pairs * tile * tile),
    )

    def remote(
        place_ref, ou_ref, oi_ref, oc_ref, up_ref, ux_ref, count_ref, utile_ref, itile_ref, uacc_in, iacc_in, w_ref,
        *refs,
    ):
        recv = refs[:peers]
        swap = refs[peers : 2 * peers]
        outs = refs[2 * peers : 2 * peers + peers + 3]
        vbuf, uacc, iacc = refs[2 * peers + peers + 3 :]
        pos = place_ref[0]
        core = lax.rem(place_ref[1], cores)
        mine = pl.multiple_of(core * half, half)
        other = pl.multiple_of((1 - core) * half, half)
        count = count_ref[...]
        for k in range(peers):
            count = count + recv[k][2 * half :].astype(f32)
            for m in range(2):
                vbuf[k, m, pl.ds(mine, half)] = recv[k][m * half : (m + 1) * half]
                vbuf[k, m, pl.ds(other, half)] = swap[k][m * half : (m + 1) * half]
        own = pl.ds(pl.multiple_of(pos * shard_rows, shard_rows), shard_rows)
        iacc[...] = jnp.zeros_like(iacc)
        iacc[1, own] = iacc_in[1]
        for b in range(item_blocks):
            total = iacc_in[0, b * tile : (b + 1) * tile]
            for u in range(user_blocks):
                t = u * item_blocks + b
                total = total + itile_ref[t] * count[t : t + 1]
            iacc[0, pl.ds(pl.multiple_of(pos * shard_rows + b * tile, tile), tile)] = total
        for u in range(user_blocks):
            total = uacc_in[0, u * tile : (u + 1) * tile]
            for b in range(item_blocks):
                t = u * item_blocks + b
                total = total + utile_ref[t] * count[t : t + 1]
            uacc[0, u * tile : (u + 1) * tile] = total
        uacc[1] = uacc_in[1]
        for k in range(peers):
            group = lax.bitwise_xor(pos, k + 1)
            for s in range(obs_slots):
                at = group * obs_slots + s
                urows = pl.ds(pl.multiple_of(ou_ref[at] * tile, tile), tile)
                brows = pl.ds(pl.multiple_of(oi_ref[at] * tile, tile), tile)
                irows = pl.ds(pl.multiple_of(group * shard_rows + oi_ref[at] * tile, tile), tile)
                used = jnp.where(s < oc_ref[group], 1.0, 0.0)
                logits = rows_by_cols(up_ref[urows], vbuf[k, 0, brows])
                imputed = rows_by_cols(ux_ref[urows], vbuf[k, 1, brows])
                g, h = observed(logits, imputed, w_ref[at], used)
                uacc[0, urows] += plain(g, vbuf[k, 0, brows])
                uacc[1, urows] += plain(h, vbuf[k, 1, brows])
                iacc[0, irows] += over_rows(g, up_ref[urows])
                iacc[1, irows] += over_rows(h, ux_ref[urows])
        for k in range(item_ways):
            rows = pl.ds(pl.multiple_of(lax.bitwise_xor(pos, k) * share, share), share)
            for m in range(2):
                part = uacc[m, rows]
                if k == 0:
                    outs[peers][m * share : (m + 1) * share] = part
                else:
                    outs[k - 1][m * share : (m + 1) * share] = part.astype(bf16)
        send, keep = outs[peers + 1], outs[peers + 2]
        for m in range(2):
            for j in range(item_ways):
                for q in range(chips):
                    at = ((m * item_ways + j) * chips + q) * item_share
                    base = j * shard_rows + q * cores * item_share
                    to_keep = pl.ds(pl.multiple_of(base + core * item_share, item_share), item_share)
                    to_send = pl.ds(pl.multiple_of(base + (1 - core) * item_share, item_share), item_share)
                    keep[at : at + item_share] = iacc[m, to_keep]
                    send[at : at + item_share] = iacc[m, to_send].astype(bf16)

    core_rows = 2 * item_ways * chips * item_share
    results = call(
        remote,
        "remote_tiles",
        tuple(shape((2 * share, rank), bf16) for _ in range(peers))
        + (shape((2 * share, rank), f32), shape((core_rows, rank), bf16), shape((core_rows, rank), f32)),
        [SM, SM, SM, SM] + [VM] * (8 + 2 * peers),
        (
            place, obs_user, obs_item, obs_count, user_pred, user_imp, own_count, utile, itile, uacc, iacc, weights,
            *received, *swapped,
        ),
        (6 * (obs_all - obs_slots) * 2 * tile**3, 8000000, 2 * (obs_all - obs_slots) * tile * tile),
        (
            pltpu.VMEM((peers, 2, shard_rows, rank), bf16),
            pltpu.VMEM((2, user_rows, rank), f32),
            pltpu.VMEM((2, item_ways * shard_rows, rank), f32),
        ),
    )
    user_own, core_send, core_keep = results[peers:]
    core_recv = core_peer(core_send)
    user_recv = [item_peer(results[k], k + 1) for k in range(peers)]

    chip_rows = 2 * item_ways * item_share

    def fold_core(place_ref, keep_ref, recv_ref, *outs):
        chip = lax.div(place_ref[1], cores)
        for k in range(chips):
            peer = lax.bitwise_xor(chip, k)
            for g in range(2 * item_ways):
                rows = pl.ds(pl.multiple_of((g * chips + peer) * item_share, item_share), item_share)
                part = keep_ref[rows] + recv_ref[rows].astype(f32)
                outs[k][g * item_share : (g + 1) * item_share] = part.astype(outs[k].dtype)

    folded = call(
        fold_core,
        "fold_core",
        (shape((chip_rows, rank), f32),) + tuple(shape((chip_rows, rank), bf16) for _ in range(chips - 1)),
        [SM, VM, VM],
        (place, core_keep, core_recv),
        (0, 1000000, 0),
    )
    chip_recv = [chip_peer(folded[k], k) for k in range(1, chips)]

    def fold_chips(place_ref, own_ref, *refs):
        recv = refs[: chips - 1]
        outs = refs[chips - 1 :]
        pos = place_ref[0]
        for k in range(item_ways):
            peer = lax.bitwise_xor(pos, k)
            for m in range(2):
                rows = pl.ds(pl.multiple_of((m * item_ways + peer) * item_share, item_share), item_share)
                part = own_ref[rows]
                for r in recv:
                    part = part + r[rows].astype(f32)
                outs[k][m * item_share : (m + 1) * item_share] = part

    shares = call(
        fold_chips,
        "fold_chips",
        tuple(shape((2 * item_share, rank), f32) for _ in range(item_ways)),
        [SM, VM] + [VM] * (chips - 1),
        (place, folded[0], *chip_recv),
        (0, 300000, 0),
    )
    item_recv = [item_peer(shares[k], k) for k in range(1, item_ways)]

    def finish(user_ref, item_ref, *refs):
        urecv = refs[:peers]
        irecv = refs[peers : 2 * peers]
        outs = refs[2 * peers :]
        for m in range(2):
            part = user_ref[m * share : (m + 1) * share]
            for r in urecv:
                part = part + r[m * share : (m + 1) * share].astype(f32)
            outs[m][...] = part
            part = item_ref[m * item_share : (m + 1) * item_share]
            for r in irecv:
                part = part + r[m * item_share : (m + 1) * item_share]
            outs[2 + m][...] = part

    return call(
        finish,
        "finish",
        (shape((share, rank), f32),) * 2 + (shape((item_share, rank), f32),) * 2,
        [VM] * (2 + 2 * peers),
        (user_own, shares[0], *user_recv, *item_recv),
        (0, 1000000, 0),
    )


def solution(mesh):
    in_specs = (
        P("user", None),
        P("user", None),
        P("item", None),
        P("item", None),
        P("user", "item", None),
        P("user", "item", None),
        P("user", "item", None),
        P("user", "item", None),
        P("user", "item", None),
        P("user", "item", None, None, None),
        P("user", "item", None, None, None),
    )
    out_specs = (
        P(("user", "item"), None),
        P(("user", "item"), None),
        P(("item", "user"), None),
        P(("item", "user"), None),
    )
    return jax.shard_map(shards, mesh=mesh, in_specs=in_specs, out_specs=out_specs, check_vma=False)
```

```python
import jax
import jax.numpy as jnp
from jax import lax
from jax.experimental import pallas as pl
from jax.experimental.pallas import tpu as pltpu
from jax.sharding import PartitionSpec as P

loss_weight = 0.015625
cores = 2
vmem_bytes = 16 * 1024 * 1024

VM = pl.BlockSpec(memory_space=pltpu.VMEM)
SM = pl.BlockSpec(memory_space=pltpu.SMEM)
HBM = pl.BlockSpec(memory_space=pltpu.HBM)


def dot(first, second, dims):
    return lax.dot_general(first, second, (dims, ((), ())), preferred_element_type=jnp.float32)


def rows_by_cols(first, second):
    return dot(first, second, ((1,), (1,)))


def plain(first, second):
    return dot(first, second, ((1,), (0,)))


def over_rows(first, second):
    return dot(first, second, ((0,), (0,)))


def call(body, name, out_shapes, specs, args, cost, scratch=()):
    return pl.pallas_call(
        body,
        out_shape=out_shapes,
        in_specs=specs,
        out_specs=tuple(VM for _ in out_shapes),
        scratch_shapes=list(scratch),
        compiler_params=pltpu.CompilerParams(vmem_limit_bytes=vmem_bytes),
        cost_estimate=pl.CostEstimate(flops=cost[0], bytes_accessed=cost[1], transcendentals=cost[2]),
        name=name,
    )(*args)


def in_hbm(arrays):
    return tuple(pltpu.with_memory_space_constraint(x, pltpu.HBM) for x in arrays)


def shape(dims, kind):
    return jax.ShapeDtypeStruct(dims, kind)


def shards(
    user_pred,
    user_imp,
    item_pred,
    item_imp,
    uno_user,
    uno_item,
    obs_user,
    obs_item,
    obs_count,
    obs_label,
    obs_prop,
):
    item_ways = lax.axis_size("item")
    user_ways = lax.axis_size("user")
    chips = user_ways // cores
    tile = obs_label.shape[-1]
    rank = user_pred.shape[1]
    user_rows = user_pred.shape[0]
    shard_rows = item_pred.shape[0]
    user_blocks = user_rows // tile
    item_blocks = shard_rows // tile
    pairs = user_blocks * item_blocks
    half = shard_rows // cores
    share = user_rows // item_ways
    item_share = shard_rows // user_ways
    uno_slots = uno_user.shape[-1] // item_ways
    obs_all = obs_user.shape[-1]
    obs_slots = obs_all // item_ways
    peers = item_ways - 1
    f32 = jnp.float32
    bf16 = jnp.bfloat16

    uno_user = uno_user.reshape(-1)
    uno_item = uno_item.reshape(-1)
    obs_user = obs_user.reshape(-1)
    obs_item = obs_item.reshape(-1)
    obs_count = obs_count.reshape(-1)
    labels = obs_label.reshape(obs_all, tile, tile)
    propens = obs_prop.reshape(obs_all, tile, tile)

    def item_peer(x, k):
        return lax.ppermute(x, "item", [(i, i ^ k) for i in range(item_ways)])

    def core_peer(x):
        return lax.ppermute(x, "user", [(i, i ^ 1) for i in range(user_ways)])

    def chip_peer(x, k):
        return lax.ppermute(x, "user", [(i, i ^ (cores * k)) for i in range(user_ways)])

    def pack(uu_hbm, ui_hbm, vp_hbm, vi_hbm, *refs):
        outs = refs[: peers + 1]
        uu_ref, ui_ref, sems, ssem = refs[peers + 1 :]
        pos = lax.axis_index("item")
        core = lax.rem(lax.axis_index("user"), cores)
        start = pl.multiple_of(core * half, half)
        lists = [
            pltpu.make_async_copy(uu_hbm, uu_ref, ssem.at[0]),
            pltpu.make_async_copy(ui_hbm, ui_ref, ssem.at[1]),
        ]
        for c in lists:
            c.start()
        copies = []
        for k in range(peers):
            for m, ref in enumerate((vp_hbm, vi_hbm)):
                copies.append(
                    pltpu.make_async_copy(
                        ref.at[pl.ds(start, half)], outs[k].at[pl.ds(m * half, half)], sems.at[k, m]
                    )
                )
        for c in copies:
            c.start()
        for c in lists:
            c.wait()
        row = lax.broadcasted_iota(jnp.int32, (pairs, rank), 0)
        for k in range(item_ways):
            group = lax.bitwise_xor(pos, k)
            count = jnp.zeros((pairs, rank), f32)
            for s in range(uno_slots):
                at = group * uno_slots + s
                pair = uu_ref[at] * item_blocks + ui_ref[at]
                count = count + jnp.where(row == pair, 1.0, 0.0)
            if k == 0:
                outs[peers][...] = count
            else:
                outs[k - 1][2 * half :] = count.astype(bf16)
        for c in copies:
            c.wait()

    packed = call(
        pack,
        "pack",
        tuple(shape((2 * half + pairs, rank), bf16) for _ in range(peers)) + (shape((pairs, rank), f32),),
        [HBM, HBM, HBM, HBM],
        in_hbm((uno_user, uno_item, item_pred, item_imp)),
        (0, 400000, 0),
        (
            pltpu.SMEM(uno_user.shape, jnp.int32),
            pltpu.SMEM(uno_item.shape, jnp.int32),
            pltpu.SemaphoreType.DMA((peers, 2)),
            pltpu.SemaphoreType.DMA((2,)),
        ),
    )
    own_count = packed[peers]
    received = [item_peer(packed[k], k + 1) for k in range(peers)]

    def observed(logits, imputed, weight, used):
        p = jax.nn.sigmoid(logits)
        q = jax.nn.sigmoid(imputed)
        miss = q - jnp.where(weight < 0, 1.0, 0.0)
        term = jnp.abs(weight) * miss
        g = (((p - q) + term) * (used * loss_weight)).astype(bf16)
        h = (2.0 * term * logits * logits * q * (1.0 - q) * (used * loss_weight)).astype(bf16)
        return g, h

    def local(ou_hbm, oi_hbm, oc_hbm, up_hbm, ux_hbm, vp_hbm, vi_hbm, lab_hbm, prop_hbm, *refs):
        utile_ref, itile_ref, uacc_ref, iacc_ref, w_ref, one_ref = refs[:6]
        bufs = refs[6:15]
        sems = refs[15]
        ou_ref, oi_ref, oc_ref, up_ref, ux_ref, vp_ref, vi_ref, lab_ref, prop_ref = bufs
        sources = (ou_hbm, oi_hbm, oc_hbm, up_hbm, ux_hbm, vp_hbm, vi_hbm, lab_hbm, prop_hbm)
        copies = [pltpu.make_async_copy(a, b, sems.at[n]) for n, (a, b) in enumerate(zip(sources, bufs))]
        for n in (5, 6, 3, 4, 0, 1, 2, 7, 8):
            copies[n].start()
        pos = lax.axis_index("item")
        one_ref[...] = jnp.ones_like(one_ref)
        uacc_ref[...] = jnp.zeros_like(uacc_ref)
        iacc_ref[...] = jnp.zeros_like(iacc_ref)
        for n in (5, 6, 3, 4):
            copies[n].wait()
        for u in range(user_blocks):
            urows = pl.ds(u * tile, tile)
            for b in range(item_blocks):
                irows = pl.ds(b * tile, tile)
                logits = rows_by_cols(up_ref[urows], vp_ref[irows])
                imputed = rows_by_cols(ux_ref[urows], vi_ref[irows])
                g = ((jax.nn.sigmoid(logits) - jax.nn.sigmoid(imputed)) * loss_weight).astype(bf16)
                utile_ref[u * item_blocks + b] = plain(g, vp_ref[irows])
                itile_ref[u * item_blocks + b] = over_rows(g, up_ref[urows])
        for n in (0, 1, 2, 7, 8):
            copies[n].wait()
        for t in range(obs_all):
            state = lab_ref[t]
            inverse = 1.0 / prop_ref[t].astype(f32)
            w_ref[t] = jnp.where(state == 0, 0.0, jnp.where(state == 2, -inverse, inverse))
        for s in range(obs_slots):
            at = pos * obs_slots + s
            urows = pl.ds(pl.multiple_of(ou_ref[at] * tile, tile), tile)
            irows = pl.ds(pl.multiple_of(oi_ref[at] * tile, tile), tile)
            used = jnp.where(s < oc_ref[pos], 1.0, 0.0)
            logits = rows_by_cols(up_ref[urows], vp_ref[irows])
            imputed = rows_by_cols(ux_ref[urows], vi_ref[irows])
            g, h = observed(logits, imputed, w_ref[at], used)
            uacc_ref[0, urows] += plain(g, vp_ref[irows])
            uacc_ref[1, urows] += plain(h, vi_ref[irows])
            iacc_ref[0, irows] += over_rows(g, up_ref[urows])
            iacc_ref[1, irows] += over_rows(h, ux_ref[urows])

    local_args = (obs_user, obs_item, obs_count, user_pred, user_imp, item_pred, item_imp, labels, propens)
    utile, itile, uacc, iacc, weights, one = call(
        local,
        "local_tiles",
        (
            shape((pairs, tile, rank), f32),
            shape((pairs, tile, rank), f32),
            shape((2, user_rows, rank), f32),
            shape((2, shard_rows, rank), f32),
            shape((obs_all, tile, tile), f32),
            shape((16, rank), bf16),
        ),
        [HBM] * 9,
        in_hbm(local_args),
        (4 * pairs * 2 * tile**3, 8000000, 2 * pairs * tile * tile),
        tuple(pltpu.SMEM(x.shape, x.dtype) for x in local_args[:3])
        + tuple(pltpu.VMEM(x.shape, x.dtype) for x in local_args[3:])
        + (pltpu.SemaphoreType.DMA((9,)),),
    )
    swapped = [core_peer(x[: 2 * half] * one[:1]) for x in received]

    def remote(
        ou_ref, oi_ref, oc_ref, up_ref, ux_ref, count_ref, utile_ref, itile_ref, uacc_in, iacc_in, w_ref, *refs
    ):
        recv = refs[:peers]
        swap = refs[peers : 2 * peers]
        outs = refs[2 * peers : 2 * peers + peers + 3]
        vbuf, uacc, iacc = refs[2 * peers + peers + 3 :]
        pos = lax.axis_index("item")
        user = lax.axis_index("user")
        core = lax.rem(user, cores)
        chip = lax.div(user, cores)
        mine = pl.multiple_of(core * half, half)
        other = pl.multiple_of((1 - core) * half, half)
        count = count_ref[...]
        for k in range(peers):
            count = count + recv[k][2 * half :].astype(f32)
            for m in range(2):
                vbuf[k, m, pl.ds(mine, half)] = recv[k][m * half : (m + 1) * half]
                vbuf[k, m, pl.ds(other, half)] = swap[k][m * half : (m + 1) * half]
        own = pl.ds(pl.multiple_of(pos * shard_rows, shard_rows), shard_rows)
        iacc[...] = jnp.zeros_like(iacc)
        iacc[1, own] = iacc_in[1]
        for b in range(item_blocks):
            total = iacc_in[0, b * tile : (b + 1) * tile]
            for u in range(user_blocks):
                t = u * item_blocks + b
                total = total + itile_ref[t] * count[t : t + 1]
            iacc[0, pl.ds(pl.multiple_of(pos * shard_rows + b * tile, tile), tile)] = total
        for u in range(user_blocks):
            total = uacc_in[0, u * tile : (u + 1) * tile]
            for b in range(item_blocks):
                t = u * item_blocks + b
                total = total + utile_ref[t] * count[t : t + 1]
            uacc[0, u * tile : (u + 1) * tile] = total
        uacc[1] = uacc_in[1]
        for k in range(peers):
            group = lax.bitwise_xor(pos, k + 1)
            for s in range(obs_slots):
                at = group * obs_slots + s
                urows = pl.ds(pl.multiple_of(ou_ref[at] * tile, tile), tile)
                brows = pl.ds(pl.multiple_of(oi_ref[at] * tile, tile), tile)
                irows = pl.ds(pl.multiple_of(group * shard_rows + oi_ref[at] * tile, tile), tile)
                used = jnp.where(s < oc_ref[group], 1.0, 0.0)
                logits = rows_by_cols(up_ref[urows], vbuf[k, 0, brows])
                imputed = rows_by_cols(ux_ref[urows], vbuf[k, 1, brows])
                g, h = observed(logits, imputed, w_ref[at], used)
                uacc[0, urows] += plain(g, vbuf[k, 0, brows])
                uacc[1, urows] += plain(h, vbuf[k, 1, brows])
                iacc[0, irows] += over_rows(g, up_ref[urows])
                iacc[1, irows] += over_rows(h, ux_ref[urows])
        for k in range(item_ways):
            rows = pl.ds(pl.multiple_of(lax.bitwise_xor(pos, k) * share, share), share)
            for m in range(2):
                part = uacc[m, rows]
                if k == 0:
                    outs[peers][m * share : (m + 1) * share] = part
                else:
                    outs[k - 1][m * share : (m + 1) * share] = part.astype(bf16)
        send, keep = outs[peers + 1], outs[peers + 2]
        for q in range(chips):
            for r in range(item_ways):
                for m in range(2):
                    at = ((q * item_ways + r) * 2 + m) * item_share
                    base = lax.bitwise_xor(pos, r) * shard_rows + lax.bitwise_xor(chip, q) * cores * item_share
                    to_keep = pl.ds(pl.multiple_of(base + core * item_share, item_share), item_share)
                    to_send = pl.ds(pl.multiple_of(base + (1 - core) * item_share, item_share), item_share)
                    keep[at : at + item_share] = iacc[m, to_keep]
                    send[at : at + item_share] = iacc[m, to_send].astype(bf16)

    core_rows = 2 * item_ways * chips * item_share
    results = call(
        remote,
        "remote_tiles",
        tuple(shape((2 * share, rank), bf16) for _ in range(peers))
        + (shape((2 * share, rank), f32), shape((core_rows, rank), bf16), shape((core_rows, rank), f32)),
        [SM, SM, SM] + [VM] * (8 + 2 * peers),
        (
            obs_user, obs_item, obs_count, user_pred, user_imp, own_count, utile, itile, uacc, iacc, weights,
            *received, *swapped,
        ),
        (6 * (obs_all - obs_slots) * 2 * tile**3, 8000000, 2 * (obs_all - obs_slots) * tile * tile),
        (
            pltpu.VMEM((peers, 2, shard_rows, rank), bf16),
            pltpu.VMEM((2, user_rows, rank), f32),
            pltpu.VMEM((2, item_ways * shard_rows, rank), f32),
        ),
    )
    user_own, core_send, core_keep = results[peers:]
    core_recv = core_peer(core_send)
    user_recv = [item_peer(results[k], k + 1) for k in range(peers)]

    chip_rows = 2 * item_ways * item_share

    def fold_core(keep_ref, recv_ref, *outs):
        for k in range(chips):
            rows = pl.ds(k * chip_rows, chip_rows)
            outs[k][...] = (keep_ref[rows] + recv_ref[rows].astype(f32)).astype(outs[k].dtype)

    folded = call(
        fold_core,
        "fold_core",
        (shape((chip_rows, rank), f32),) + tuple(shape((chip_rows, rank), bf16) for _ in range(chips - 1)),
        [VM, VM],
        (core_keep, core_recv),
        (0, 1000, 0),
    )
    chip_recv = [chip_peer(folded[k], k) for k in range(1, chips)]

    def fold_chips(own_ref, *refs):
        recv = refs[: chips - 1]
        outs = refs[chips - 1 :]
        for k in range(item_ways):
            rows = pl.ds(k * 2 * item_share, 2 * item_share)
            part = own_ref[rows]
            for r in recv:
                part = part + r[rows].astype(f32)
            outs[k][...] = part

    shares = call(
        fold_chips,
        "fold_chips",
        tuple(shape((2 * item_share, rank), f32) for _ in range(item_ways)),
        [VM] * chips,
        (folded[0], *chip_recv),
        (0, 1000, 0),
    )
    item_recv = [item_peer(shares[k], k) for k in range(1, item_ways)]

    def finish(user_ref, item_ref, *refs):
        urecv = refs[:peers]
        irecv = refs[peers : 2 * peers]
        outs = refs[2 * peers :]
        for m in range(2):
            part = user_ref[m * share : (m + 1) * share]
            for r in urecv:
                part = part + r[m * share : (m + 1) * share].astype(f32)
            outs[m][...] = part
            part = item_ref[m * item_share : (m + 1) * item_share]
            for r in irecv:
                part = part + r[m * item_share : (m + 1) * item_share]
            outs[2 + m][...] = part

    return call(
        finish,
        "finish",
        (shape((share, rank), f32),) * 2 + (shape((item_share, rank), f32),) * 2,
        [VM] * (2 + 2 * peers),
        (user_own, shares[0], *user_recv, *item_recv),
        (0, 1000000, 0),
    )


def solution(mesh):
    in_specs = (
        P("user", None),
        P("user", None),
        P("item", None),
        P("item", None),
        P("user", "item", None),
        P("user", "item", None),
        P("user", "item", None),
        P("user", "item", None),
        P("user", "item", None),
        P("user", "item", None, None, None),
        P("user", "item", None, None, None),
    )
    out_specs = (
        P(("user", "item"), None),
        P(("user", "item"), None),
        P(("item", "user"), None),
        P(("item", "user"), None),
    )
    return jax.shard_map(shards, mesh=mesh, in_specs=in_specs, out_specs=out_specs, check_vma=False)
```

```python
import jax
import jax.numpy as jnp
from jax import lax
from jax.experimental import pallas as pl
from jax.experimental.pallas import tpu as pltpu
from jax.sharding import PartitionSpec as P

loss_weight = 0.015625
cores = 2
vmem_bytes = 16 * 1024 * 1024

VM = pl.BlockSpec(memory_space=pltpu.VMEM)
SM = pl.BlockSpec(memory_space=pltpu.SMEM)
HBM = pl.BlockSpec(memory_space=pltpu.HBM)


def dot(first, second, dims):
    return lax.dot_general(first, second, (dims, ((), ())), preferred_element_type=jnp.float32)


def rows_by_cols(first, second):
    return dot(first, second, ((1,), (1,)))


def plain(first, second):
    return dot(first, second, ((1,), (0,)))


def over_rows(first, second):
    return dot(first, second, ((0,), (0,)))


def call(body, name, out_shapes, specs, args, cost, scratch=()):
    return pl.pallas_call(
        body,
        out_shape=out_shapes,
        in_specs=specs,
        out_specs=tuple(VM for _ in out_shapes),
        scratch_shapes=list(scratch),
        compiler_params=pltpu.CompilerParams(vmem_limit_bytes=vmem_bytes),
        cost_estimate=pl.CostEstimate(flops=cost[0], bytes_accessed=cost[1], transcendentals=cost[2]),
        name=name,
    )(*args)


def in_hbm(arrays):
    return tuple(pltpu.with_memory_space_constraint(x, pltpu.HBM) for x in arrays)


def shape(dims, kind):
    return jax.ShapeDtypeStruct(dims, kind)


def shards(
    user_pred,
    user_imp,
    item_pred,
    item_imp,
    uno_user,
    uno_item,
    obs_user,
    obs_item,
    obs_count,
    obs_label,
    obs_prop,
):
    item_ways = lax.axis_size("item")
    user_ways = lax.axis_size("user")
    chips = user_ways // cores
    tile = obs_label.shape[-1]
    rank = user_pred.shape[1]
    user_rows = user_pred.shape[0]
    shard_rows = item_pred.shape[0]
    user_blocks = user_rows // tile
    item_blocks = shard_rows // tile
    pairs = user_blocks * item_blocks
    half = shard_rows // cores
    share = user_rows // item_ways
    item_share = shard_rows // user_ways
    uno_slots = uno_user.shape[-1] // item_ways
    obs_all = obs_user.shape[-1]
    obs_slots = obs_all // item_ways
    peers = item_ways - 1
    f32 = jnp.float32
    bf16 = jnp.bfloat16

    uno_user = uno_user.reshape(-1)
    uno_item = uno_item.reshape(-1)
    obs_user = obs_user.reshape(-1)
    obs_item = obs_item.reshape(-1)
    obs_count = obs_count.reshape(-1)
    labels = obs_label.reshape(obs_all, tile, tile)
    propens = obs_prop.reshape(obs_all, tile, tile)

    def item_peer(x, k):
        return lax.ppermute(x, "item", [(i, i ^ k) for i in range(item_ways)])

    def core_peer(x):
        return lax.ppermute(x, "user", [(i, i ^ 1) for i in range(user_ways)])

    def chip_peer(x, k):
        return lax.ppermute(x, "user", [(i, i ^ (cores * k)) for i in range(user_ways)])

    def pack(uu_hbm, ui_hbm, vp_hbm, vi_hbm, *refs):
        outs = refs[: peers + 1]
        uu_ref, ui_ref, sems, ssem = refs[peers + 1 :]
        pos = lax.axis_index("item")
        core = lax.rem(lax.axis_index("user"), cores)
        start = pl.multiple_of(core * half, half)
        lists = [
            pltpu.make_async_copy(uu_hbm, uu_ref, ssem.at[0]),
            pltpu.make_async_copy(ui_hbm, ui_ref, ssem.at[1]),
        ]
        for c in lists:
            c.start()
        copies = []
        for k in range(peers):
            for m, ref in enumerate((vp_hbm, vi_hbm)):
                copies.append(
                    pltpu.make_async_copy(
                        ref.at[pl.ds(start, half)], outs[k].at[pl.ds(m * half, half)], sems.at[k, m]
                    )
                )
        for c in copies:
            c.start()
        for c in lists:
            c.wait()
        row = lax.broadcasted_iota(jnp.int32, (pairs, rank), 0)
        for k in range(item_ways):
            group = lax.bitwise_xor(pos, k)
            count = jnp.zeros((pairs, rank), f32)
            for s in range(uno_slots):
                at = group * uno_slots + s
                pair = uu_ref[at] * item_blocks + ui_ref[at]
                count = count + jnp.where(row == pair, 1.0, 0.0)
            if k == 0:
                outs[peers][...] = count
            else:
                outs[k - 1][2 * half :] = count.astype(bf16)
        for c in copies:
            c.wait()

    packed = call(
        pack,
        "pack",
        tuple(shape((2 * half + pairs, rank), bf16) for _ in range(peers)) + (shape((pairs, rank), f32),),
        [HBM, HBM, HBM, HBM],
        in_hbm((uno_user, uno_item, item_pred, item_imp)),
        (0, 400000, 0),
        (
            pltpu.SMEM(uno_user.shape, jnp.int32),
            pltpu.SMEM(uno_item.shape, jnp.int32),
            pltpu.SemaphoreType.DMA((peers, 2)),
            pltpu.SemaphoreType.DMA((2,)),
        ),
    )
    own_count = packed[peers]
    received = [item_peer(packed[k], k + 1) for k in range(peers)]

    def observed(logits, imputed, weight, used):
        p = jax.nn.sigmoid(logits)
        q = jax.nn.sigmoid(imputed)
        miss = q - jnp.where(weight < 0, 1.0, 0.0)
        term = jnp.abs(weight) * miss
        g = (((p - q) + term) * (used * loss_weight)).astype(bf16)
        h = (2.0 * term * logits * logits * q * (1.0 - q) * (used * loss_weight)).astype(bf16)
        return g, h

    def local(ou_hbm, oi_hbm, oc_hbm, up_hbm, ux_hbm, vp_hbm, vi_hbm, lab_hbm, prop_hbm, *refs):
        utile_ref, itile_ref, uacc_ref, iacc_ref, w_ref = refs[:5]
        ones = refs[5 : 5 + peers]
        bufs = refs[5 + peers : 14 + peers]
        sems, gbuf, hbuf = refs[14 + peers :]
        ou_ref, oi_ref, oc_ref, up_ref, ux_ref, vp_ref, vi_ref, lab_ref, prop_ref = bufs
        sources = (ou_hbm, oi_hbm, oc_hbm, up_hbm, ux_hbm, vp_hbm, vi_hbm, lab_hbm, prop_hbm)
        copies = [pltpu.make_async_copy(a, b, sems.at[n]) for n, (a, b) in enumerate(zip(sources, bufs))]
        for n in (5, 6, 3, 4, 0, 1, 2, 7, 8):
            copies[n].start()
        pos = lax.axis_index("item")
        for ref in ones:
            ref[...] = jnp.ones_like(ref)
        uacc_ref[...] = jnp.zeros_like(uacc_ref)
        iacc_ref[...] = jnp.zeros_like(iacc_ref)
        for n in (5, 6, 3, 4):
            copies[n].wait()
        for u in range(user_blocks):
            urows = pl.ds(u * tile, tile)
            for b in range(item_blocks):
                irows = pl.ds(b * tile, tile)
                logits = rows_by_cols(up_ref[urows], vp_ref[irows])
                imputed = rows_by_cols(ux_ref[urows], vi_ref[irows])
                gbuf[u * item_blocks + b] = (
                    (jax.nn.sigmoid(logits) - jax.nn.sigmoid(imputed)) * loss_weight
                ).astype(bf16)
        for n in (0, 1, 2, 7, 8):
            copies[n].wait()
        for t in range(obs_all):
            state = lab_ref[t]
            inverse = 1.0 / prop_ref[t].astype(f32)
            w_ref[t] = jnp.where(state == 0, 0.0, jnp.where(state == 2, -inverse, inverse))
        places = []
        for s in range(obs_slots):
            at = pos * obs_slots + s
            urows = pl.ds(pl.multiple_of(ou_ref[at] * tile, tile), tile)
            irows = pl.ds(pl.multiple_of(oi_ref[at] * tile, tile), tile)
            places.append((urows, irows))
            used = jnp.where(s < oc_ref[pos], 1.0, 0.0)
            logits = rows_by_cols(up_ref[urows], vp_ref[irows])
            imputed = rows_by_cols(ux_ref[urows], vi_ref[irows])
            gbuf[pairs + s], hbuf[s] = observed(logits, imputed, w_ref[at], used)
        for u in range(user_blocks):
            urows = pl.ds(u * tile, tile)
            for b in range(item_blocks):
                t = u * item_blocks + b
                utile_ref[t] = plain(gbuf[t], vp_ref[b * tile : (b + 1) * tile])
                itile_ref[t] = over_rows(gbuf[t], up_ref[urows])
        for s, (urows, irows) in enumerate(places):
            uacc_ref[0, urows] += plain(gbuf[pairs + s], vp_ref[irows])
            uacc_ref[1, urows] += plain(hbuf[s], vi_ref[irows])
            iacc_ref[0, irows] += over_rows(gbuf[pairs + s], up_ref[urows])
            iacc_ref[1, irows] += over_rows(hbuf[s], ux_ref[urows])

    local_args = (obs_user, obs_item, obs_count, user_pred, user_imp, item_pred, item_imp, labels, propens)
    utile, itile, uacc, iacc, weights, *ones = call(
        local,
        "local_tiles",
        (
            shape((pairs, tile, rank), f32),
            shape((pairs, tile, rank), f32),
            shape((2, user_rows, rank), f32),
            shape((2, shard_rows, rank), f32),
            shape((obs_all, tile, tile), f32),
            *(shape((16, rank), bf16) for _ in range(peers)),
        ),
        [HBM] * 9,
        in_hbm(local_args),
        (4 * pairs * 2 * tile**3, 8000000, 2 * pairs * tile * tile),
        tuple(pltpu.SMEM(x.shape, x.dtype) for x in local_args[:3])
        + tuple(pltpu.VMEM(x.shape, x.dtype) for x in local_args[3:])
        + (
            pltpu.SemaphoreType.DMA((9,)),
            pltpu.VMEM((pairs + obs_slots, tile, tile), bf16),
            pltpu.VMEM((obs_slots, tile, tile), bf16),
        ),
    )
    swapped = [core_peer(x[: 2 * half] * one[:1]) for x, one in zip(received, ones)]

    slots = peers * obs_slots

    def items(ou_hbm, oi_hbm, oc_hbm, up_ref, ux_ref, count_ref, itile_ref, iacc_in, w_ref, *refs):
        recv = refs[:peers]
        swap = refs[peers : 2 * peers]
        send, keep, vbuf, gbuf, hbuf, total_ref = refs[2 * peers : 2 * peers + 6]
        ou_ref, oi_ref, oc_ref, sems, iacc = refs[2 * peers + 6 :]
        copies = [
            pltpu.make_async_copy(ou_hbm, ou_ref, sems.at[0]),
            pltpu.make_async_copy(oi_hbm, oi_ref, sems.at[1]),
            pltpu.make_async_copy(oc_hbm, oc_ref, sems.at[2]),
        ]
        for c in copies:
            c.start()
        pos = lax.axis_index("item")
        user = lax.axis_index("user")
        core = lax.rem(user, cores)
        chip = lax.div(user, cores)
        mine = pl.multiple_of(core * half, half)
        other = pl.multiple_of((1 - core) * half, half)
        count = count_ref[...]
        for k in range(peers):
            count = count + recv[k][2 * half :].astype(f32)
            for m in range(2):
                vbuf[k, m, pl.ds(mine, half)] = recv[k][m * half : (m + 1) * half]
                vbuf[k, m, pl.ds(other, half)] = swap[k][m * half : (m + 1) * half]
        total_ref[...] = count
        own = pl.ds(pl.multiple_of(pos * shard_rows, shard_rows), shard_rows)
        iacc[...] = jnp.zeros_like(iacc)
        iacc[1, own] = iacc_in[1]
        for b in range(item_blocks):
            total = iacc_in[0, b * tile : (b + 1) * tile]
            for u in range(user_blocks):
                t = u * item_blocks + b
                total = total + itile_ref[t] * count[t : t + 1]
            iacc[0, pl.ds(pl.multiple_of(pos * shard_rows + b * tile, tile), tile)] = total
        for c in copies:
            c.wait()
        places = []
        for k in range(peers):
            group = lax.bitwise_xor(pos, k + 1)
            for s in range(obs_slots):
                at = group * obs_slots + s
                urows = pl.ds(pl.multiple_of(ou_ref[at] * tile, tile), tile)
                brows = pl.ds(pl.multiple_of(oi_ref[at] * tile, tile), tile)
                irows = pl.ds(pl.multiple_of(group * shard_rows + oi_ref[at] * tile, tile), tile)
                places.append((urows, irows))
                used = jnp.where(s < oc_ref[group], 1.0, 0.0)
                logits = rows_by_cols(up_ref[urows], vbuf[k, 0, brows])
                imputed = rows_by_cols(ux_ref[urows], vbuf[k, 1, brows])
                t = k * obs_slots + s
                gbuf[t], hbuf[t] = observed(logits, imputed, w_ref[at], used)
        for t, (urows, irows) in enumerate(places):
            iacc[0, irows] += over_rows(gbuf[t], up_ref[urows])
            iacc[1, irows] += over_rows(hbuf[t], ux_ref[urows])
        for q in range(chips):
            for r in range(item_ways):
                for m in range(2):
                    at = ((q * item_ways + r) * 2 + m) * item_share
                    base = lax.bitwise_xor(pos, r) * shard_rows + lax.bitwise_xor(chip, q) * cores * item_share
                    to_keep = pl.ds(pl.multiple_of(base + core * item_share, item_share), item_share)
                    to_send = pl.ds(pl.multiple_of(base + (1 - core) * item_share, item_share), item_share)
                    keep[at : at + item_share] = iacc[m, to_keep]
                    send[at : at + item_share] = iacc[m, to_send].astype(bf16)

    core_rows = 2 * item_ways * chips * item_share
    id_args = (obs_user, obs_item, obs_count)
    core_send, core_keep, vbuf, gbuf, hbuf, count = call(
        items,
        "item_tiles",
        (
            shape((core_rows, rank), bf16),
            shape((core_rows, rank), f32),
            shape((peers, 2, shard_rows, rank), bf16),
            shape((slots, tile, tile), bf16),
            shape((slots, tile, tile), bf16),
            shape((pairs, rank), f32),
        ),
        [HBM, HBM, HBM] + [VM] * (6 + 2 * peers),
        (*in_hbm(id_args), user_pred, user_imp, own_count, itile, iacc, weights, *received, *swapped),
        (4 * slots * 2 * tile**3, 4000000, 2 * slots * tile * tile),
        tuple(pltpu.SMEM(x.shape, x.dtype) for x in id_args)
        + (pltpu.SemaphoreType.DMA((3,)), pltpu.VMEM((2, item_ways * shard_rows, rank), f32)),
    )

    def users(ou_hbm, oi_hbm, utile_ref, uacc_in, count_ref, vbuf, gbuf, hbuf, *refs):
        outs = refs[: peers + 1]
        ou_ref, oi_ref, sems, uacc = refs[peers + 1 :]
        copies = [
            pltpu.make_async_copy(ou_hbm, ou_ref, sems.at[0]),
            pltpu.make_async_copy(oi_hbm, oi_ref, sems.at[1]),
        ]
        for c in copies:
            c.start()
        pos = lax.axis_index("item")
        count = count_ref[...]
        for u in range(user_blocks):
            total = uacc_in[0, u * tile : (u + 1) * tile]
            for b in range(item_blocks):
                t = u * item_blocks + b
                total = total + utile_ref[t] * count[t : t + 1]
            uacc[0, u * tile : (u + 1) * tile] = total
        uacc[1] = uacc_in[1]
        for c in copies:
            c.wait()
        for k in range(peers):
            group = lax.bitwise_xor(pos, k + 1)
            for s in range(obs_slots):
                at = group * obs_slots + s
                t = k * obs_slots + s
                urows = pl.ds(pl.multiple_of(ou_ref[at] * tile, tile), tile)
                brows = pl.ds(pl.multiple_of(oi_ref[at] * tile, tile), tile)
                uacc[0, urows] += plain(gbuf[t], vbuf[k, 0, brows])
                uacc[1, urows] += plain(hbuf[t], vbuf[k, 1, brows])
        for k in range(item_ways):
            rows = pl.ds(pl.multiple_of(lax.bitwise_xor(pos, k) * share, share), share)
            for m in range(2):
                part = uacc[m, rows]
                if k == 0:
                    outs[peers][m * share : (m + 1) * share] = part
                else:
                    outs[k - 1][m * share : (m + 1) * share] = part.astype(bf16)

    results = call(
        users,
        "user_tiles",
        tuple(shape((2 * share, rank), bf16) for _ in range(peers)) + (shape((2 * share, rank), f32),),
        [HBM, HBM] + [VM] * 6,
        (*in_hbm(id_args[:2]), utile, uacc, count, vbuf, gbuf, hbuf),
        (2 * slots * 2 * tile**3, 4000000, 0),
        tuple(pltpu.SMEM(x.shape, x.dtype) for x in id_args[:2])
        + (pltpu.SemaphoreType.DMA((2,)), pltpu.VMEM((2, user_rows, rank), f32)),
    )
    user_own = results[peers]
    core_recv = core_peer(core_send)
    user_recv = [item_peer(results[k], k + 1) for k in range(peers)]

    chip_rows = 2 * item_ways * item_share

    def fold_half(keep_ref, recv_ref, *refs):
        low_ref, high_ref = refs[-2:]
        rows = low_ref.shape[0]
        low_ref[...] = keep_ref[:rows] + recv_ref[:rows].astype(f32)
        high_ref[...] = (keep_ref[rows:] + recv_ref[rows:].astype(f32)).astype(bf16)

    kept, arrived, after = core_keep, core_recv, (user_own,)
    step = chips // 2
    while step:
        kept, sent = call(
            fold_half,
            "fold_half",
            (shape((step * chip_rows, rank), f32), shape((step * chip_rows, rank), bf16)),
            [VM, VM] + [VM] * len(after),
            (kept, arrived, *after),
            (0, 1000, 0),
        )
        arrived, after = chip_peer(sent, step), ()
        step //= 2

    def fold_chips(own_ref, recv_ref, *outs):
        for k in range(item_ways):
            rows = pl.ds(k * 2 * item_share, 2 * item_share)
            outs[k][...] = (own_ref[rows] + recv_ref[rows].astype(f32)).astype(outs[k].dtype)

    shares = call(
        fold_chips,
        "fold_chips",
        (shape((2 * item_share, rank), f32),) + tuple(shape((2 * item_share, rank), bf16) for _ in range(peers)),
        [VM, VM],
        (kept, arrived),
        (0, 1000, 0),
    )
    item_recv = [item_peer(shares[k], k) for k in range(1, item_ways)]

    def finish(user_ref, item_ref, *refs):
        urecv = refs[:peers]
        irecv = refs[peers : 2 * peers]
        outs = refs[2 * peers :]
        for m in range(2):
            part = user_ref[m * share : (m + 1) * share]
            for r in urecv:
                part = part + r[m * share : (m + 1) * share].astype(f32)
            outs[m][...] = part
            part = item_ref[m * item_share : (m + 1) * item_share]
            for r in irecv:
                part = part + r[m * item_share : (m + 1) * item_share].astype(f32)
            outs[2 + m][...] = part

    return call(
        finish,
        "finish",
        (shape((share, rank), f32),) * 2 + (shape((item_share, rank), f32),) * 2,
        [VM] * (2 + 2 * peers),
        (user_own, shares[0], *user_recv, *item_recv),
        (0, 1000000, 0),
    )


def solution(mesh):
    in_specs = (
        P("user", None),
        P("user", None),
        P("item", None),
        P("item", None),
        P("user", "item", None),
        P("user", "item", None),
        P("user", "item", None),
        P("user", "item", None),
        P("user", "item", None),
        P("user", "item", None, None, None),
        P("user", "item", None, None, None),
    )
    out_specs = (
        P(("user", "item"), None),
        P(("user", "item"), None),
        P(("item", "user"), None),
        P(("item", "user"), None),
    )
    return jax.shard_map(shards, mesh=mesh, in_specs=in_specs, out_specs=out_specs, check_vma=False)
```

```python
import jax
import jax.numpy as jnp
from jax import lax
from jax.experimental import pallas as pl
from jax.experimental.pallas import tpu as pltpu
from jax.sharding import PartitionSpec as P

loss_weight = 0.015625
cores = 2
vmem_bytes = 16 * 1024 * 1024

VM = pl.BlockSpec(memory_space=pltpu.VMEM)
SM = pl.BlockSpec(memory_space=pltpu.SMEM)
HBM = pl.BlockSpec(memory_space=pltpu.HBM)


def dot(first, second, dims):
    return lax.dot_general(first, second, (dims, ((), ())), preferred_element_type=jnp.float32)


def rows_by_cols(first, second):
    return dot(first, second, ((1,), (1,)))


def plain(first, second):
    return dot(first, second, ((1,), (0,)))


def over_rows(first, second):
    return dot(first, second, ((0,), (0,)))


def call(body, name, out_shapes, specs, args, cost, scratch=()):
    return pl.pallas_call(
        body,
        out_shape=out_shapes,
        in_specs=specs,
        out_specs=tuple(VM for _ in out_shapes),
        scratch_shapes=list(scratch),
        compiler_params=pltpu.CompilerParams(vmem_limit_bytes=vmem_bytes),
        cost_estimate=pl.CostEstimate(flops=cost[0], bytes_accessed=cost[1], transcendentals=cost[2]),
        name=name,
    )(*args)


def in_hbm(arrays):
    return tuple(pltpu.with_memory_space_constraint(x, pltpu.HBM) for x in arrays)


def shape(dims, kind):
    return jax.ShapeDtypeStruct(dims, kind)


def shards(
    user_pred,
    user_imp,
    item_pred,
    item_imp,
    uno_user,
    uno_item,
    obs_user,
    obs_item,
    obs_count,
    obs_label,
    obs_prop,
):
    item_ways = lax.axis_size("item")
    user_ways = lax.axis_size("user")
    chips = user_ways // cores
    tile = obs_label.shape[-1]
    rank = user_pred.shape[1]
    user_rows = user_pred.shape[0]
    shard_rows = item_pred.shape[0]
    user_blocks = user_rows // tile
    item_blocks = shard_rows // tile
    pairs = user_blocks * item_blocks
    half = shard_rows // cores
    share = user_rows // item_ways
    item_share = shard_rows // user_ways
    uno_slots = uno_user.shape[-1] // item_ways
    obs_all = obs_user.shape[-1]
    obs_slots = obs_all // item_ways
    peers = item_ways - 1
    f32 = jnp.float32
    bf16 = jnp.bfloat16

    uno_user = uno_user.reshape(-1)
    uno_item = uno_item.reshape(-1)
    obs_user = obs_user.reshape(-1)
    obs_item = obs_item.reshape(-1)
    obs_count = obs_count.reshape(-1)
    labels = obs_label.reshape(obs_all, tile, tile)
    propens = obs_prop.reshape(obs_all, tile, tile)

    def item_peer(x, k):
        return lax.ppermute(x, "item", [(i, i ^ k) for i in range(item_ways)])

    def core_peer(x):
        return lax.ppermute(x, "user", [(i, i ^ 1) for i in range(user_ways)])

    def chip_peer(x, k):
        return lax.ppermute(x, "user", [(i, i ^ (cores * k)) for i in range(user_ways)])

    def pack(uu_hbm, ui_hbm, vp_hbm, vi_hbm, *refs):
        outs = refs[: peers + 1]
        uu_ref, ui_ref, sems, ssem = refs[peers + 1 :]
        pos = lax.axis_index("item")
        core = lax.rem(lax.axis_index("user"), cores)
        start = pl.multiple_of(core * half, half)
        lists = [
            pltpu.make_async_copy(uu_hbm, uu_ref, ssem.at[0]),
            pltpu.make_async_copy(ui_hbm, ui_ref, ssem.at[1]),
        ]
        for c in lists:
            c.start()
        copies = []
        for k in range(peers):
            for m, ref in enumerate((vp_hbm, vi_hbm)):
                copies.append(
                    pltpu.make_async_copy(
                        ref.at[pl.ds(start, half)], outs[k].at[pl.ds(m * half, half)], sems.at[k, m]
                    )
                )
        for c in copies:
            c.start()
        for c in lists:
            c.wait()
        row = lax.broadcasted_iota(jnp.int32, (pairs, rank), 0)
        for k in range(item_ways):
            group = lax.bitwise_xor(pos, k)
            count = jnp.zeros((pairs, rank), f32)
            for s in range(uno_slots):
                at = group * uno_slots + s
                pair = uu_ref[at] * item_blocks + ui_ref[at]
                count = count + jnp.where(row == pair, 1.0, 0.0)
            if k == 0:
                outs[peers][...] = count
            else:
                outs[k - 1][2 * half :] = count.astype(bf16)
        for c in copies:
            c.wait()

    packed = call(
        pack,
        "pack",
        tuple(shape((2 * half + pairs, rank), bf16) for _ in range(peers)) + (shape((pairs, rank), f32),),
        [HBM, HBM, HBM, HBM],
        in_hbm((uno_user, uno_item, item_pred, item_imp)),
        (0, 400000, 0),
        (
            pltpu.SMEM(uno_user.shape, jnp.int32),
            pltpu.SMEM(uno_item.shape, jnp.int32),
            pltpu.SemaphoreType.DMA((peers, 2)),
            pltpu.SemaphoreType.DMA((2,)),
        ),
    )
    own_count = packed[peers]
    received = [item_peer(packed[k], k + 1) for k in reversed(range(peers))][::-1]

    def observed(logits, imputed, weight, used):
        p = jax.nn.sigmoid(logits)
        q = jax.nn.sigmoid(imputed)
        miss = q - jnp.where(weight < 0, 1.0, 0.0)
        term = jnp.abs(weight) * miss
        g = (((p - q) + term) * (used * loss_weight)).astype(bf16)
        h = (2.0 * term * logits * logits * q * (1.0 - q) * (used * loss_weight)).astype(bf16)
        return g, h

    def local(ou_hbm, oi_hbm, oc_hbm, up_hbm, ux_hbm, vp_hbm, vi_hbm, lab_hbm, prop_hbm, *refs):
        utile_ref, itile_ref, uacc_ref, iacc_ref, w_ref = refs[:5]
        ones = refs[5 : 5 + peers]
        bufs = refs[5 + peers : 14 + peers]
        sems, gbuf, hbuf = refs[14 + peers :]
        ou_ref, oi_ref, oc_ref, up_ref, ux_ref, vp_ref, vi_ref, lab_ref, prop_ref = bufs
        sources = (ou_hbm, oi_hbm, oc_hbm, up_hbm, ux_hbm, vp_hbm, vi_hbm, lab_hbm, prop_hbm)
        copies = [pltpu.make_async_copy(a, b, sems.at[n]) for n, (a, b) in enumerate(zip(sources, bufs))]
        for n in (5, 6, 3, 4, 0, 1, 2, 7, 8):
            copies[n].start()
        pos = lax.axis_index("item")
        for ref in ones:
            ref[...] = jnp.ones_like(ref)
        uacc_ref[...] = jnp.zeros_like(uacc_ref)
        iacc_ref[...] = jnp.zeros_like(iacc_ref)
        for n in (5, 6, 3, 4):
            copies[n].wait()
        for u in range(user_blocks):
            urows = pl.ds(u * tile, tile)
            for b in range(item_blocks):
                irows = pl.ds(b * tile, tile)
                logits = rows_by_cols(up_ref[urows], vp_ref[irows])
                imputed = rows_by_cols(ux_ref[urows], vi_ref[irows])
                gbuf[u * item_blocks + b] = (
                    (jax.nn.sigmoid(logits) - jax.nn.sigmoid(imputed)) * loss_weight
                ).astype(bf16)
        for n in (0, 1, 2, 7, 8):
            copies[n].wait()
        for t in range(obs_all):
            state = lab_ref[t]
            inverse = 1.0 / prop_ref[t].astype(f32)
            w_ref[t] = jnp.where(state == 0, 0.0, jnp.where(state == 2, -inverse, inverse))
        places = []
        for s in range(obs_slots):
            at = pos * obs_slots + s
            urows = pl.ds(pl.multiple_of(ou_ref[at] * tile, tile), tile)
            irows = pl.ds(pl.multiple_of(oi_ref[at] * tile, tile), tile)
            places.append((urows, irows))
            used = jnp.where(s < oc_ref[pos], 1.0, 0.0)
            logits = rows_by_cols(up_ref[urows], vp_ref[irows])
            imputed = rows_by_cols(ux_ref[urows], vi_ref[irows])
            gbuf[pairs + s], hbuf[s] = observed(logits, imputed, w_ref[at], used)
        for u in range(user_blocks):
            urows = pl.ds(u * tile, tile)
            for b in range(item_blocks):
                t = u * item_blocks + b
                utile_ref[t] = plain(gbuf[t], vp_ref[b * tile : (b + 1) * tile])
                itile_ref[t] = over_rows(gbuf[t], up_ref[urows])
        for s, (urows, irows) in enumerate(places):
            uacc_ref[0, urows] += plain(gbuf[pairs + s], vp_ref[irows])
            uacc_ref[1, urows] += plain(hbuf[s], vi_ref[irows])
            iacc_ref[0, irows] += over_rows(gbuf[pairs + s], up_ref[urows])
            iacc_ref[1, irows] += over_rows(hbuf[s], ux_ref[urows])

    local_args = (obs_user, obs_item, obs_count, user_pred, user_imp, item_pred, item_imp, labels, propens)
    utile, itile, uacc, iacc, weights, *ones = call(
        local,
        "local_tiles",
        (
            shape((pairs, tile, rank), f32),
            shape((pairs, tile, rank), f32),
            shape((2, user_rows, rank), f32),
            shape((2, shard_rows, rank), f32),
            shape((obs_all, tile, tile), f32),
            *(shape((16, rank), bf16) for _ in range(peers)),
        ),
        [HBM] * 9,
        in_hbm(local_args),
        (4 * pairs * 2 * tile**3, 8000000, 2 * pairs * tile * tile),
        tuple(pltpu.SMEM(x.shape, x.dtype) for x in local_args[:3])
        + tuple(pltpu.VMEM(x.shape, x.dtype) for x in local_args[3:])
        + (
            pltpu.SemaphoreType.DMA((9,)),
            pltpu.VMEM((pairs + obs_slots, tile, tile), bf16),
            pltpu.VMEM((obs_slots, tile, tile), bf16),
        ),
    )
    swapped = [core_peer(x[: 2 * half] * one[:1]) for x, one in zip(received[::-1], ones)][::-1]

    slots = peers * obs_slots

    def items(ou_hbm, oi_hbm, oc_hbm, up_ref, ux_ref, count_ref, itile_ref, iacc_in, w_ref, *refs):
        recv = refs[:peers][::-1]
        swap = refs[peers : 2 * peers][::-1]
        send, keep, vbuf, gbuf, hbuf, total_ref = refs[2 * peers : 2 * peers + 6]
        ou_ref, oi_ref, oc_ref, sems, iacc = refs[2 * peers + 6 :]
        copies = [
            pltpu.make_async_copy(ou_hbm, ou_ref, sems.at[0]),
            pltpu.make_async_copy(oi_hbm, oi_ref, sems.at[1]),
            pltpu.make_async_copy(oc_hbm, oc_ref, sems.at[2]),
        ]
        for c in copies:
            c.start()
        pos = lax.axis_index("item")
        user = lax.axis_index("user")
        core = lax.rem(user, cores)
        chip = lax.div(user, cores)
        mine = pl.multiple_of(core * half, half)
        other = pl.multiple_of((1 - core) * half, half)
        count = count_ref[...]
        for k in range(peers):
            count = count + recv[k][2 * half :].astype(f32)
            for m in range(2):
                vbuf[k, m, pl.ds(mine, half)] = recv[k][m * half : (m + 1) * half]
                vbuf[k, m, pl.ds(other, half)] = swap[k][m * half : (m + 1) * half]
        total_ref[...] = count
        own = pl.ds(pl.multiple_of(pos * shard_rows, shard_rows), shard_rows)
        iacc[...] = jnp.zeros_like(iacc)
        iacc[1, own] = iacc_in[1]
        for b in range(item_blocks):
            total = iacc_in[0, b * tile : (b + 1) * tile]
            for u in range(user_blocks):
                t = u * item_blocks + b
                total = total + itile_ref[t] * count[t : t + 1]
            iacc[0, pl.ds(pl.multiple_of(pos * shard_rows + b * tile, tile), tile)] = total
        for c in copies:
            c.wait()
        places = []
        for k in range(peers):
            group = lax.bitwise_xor(pos, k + 1)
            for s in range(obs_slots):
                at = group * obs_slots + s
                urows = pl.ds(pl.multiple_of(ou_ref[at] * tile, tile), tile)
                brows = pl.ds(pl.multiple_of(oi_ref[at] * tile, tile), tile)
                irows = pl.ds(pl.multiple_of(group * shard_rows + oi_ref[at] * tile, tile), tile)
                places.append((urows, irows))
                used = jnp.where(s < oc_ref[group], 1.0, 0.0)
                logits = rows_by_cols(up_ref[urows], vbuf[k, 0, brows])
                imputed = rows_by_cols(ux_ref[urows], vbuf[k, 1, brows])
                t = k * obs_slots + s
                gbuf[t], hbuf[t] = observed(logits, imputed, w_ref[at], used)
        for t, (urows, irows) in enumerate(places):
            iacc[0, irows] += over_rows(gbuf[t], up_ref[urows])
            iacc[1, irows] += over_rows(hbuf[t], ux_ref[urows])
        for q in range(chips):
            for r in range(item_ways):
                for m in range(2):
                    at = ((q * item_ways + r) * 2 + m) * item_share
                    base = lax.bitwise_xor(pos, r) * shard_rows + lax.bitwise_xor(chip, q) * cores * item_share
                    to_keep = pl.ds(pl.multiple_of(base + core * item_share, item_share), item_share)
                    to_send = pl.ds(pl.multiple_of(base + (1 - core) * item_share, item_share), item_share)
                    keep[at : at + item_share] = iacc[m, to_keep]
                    send[at : at + item_share] = iacc[m, to_send].astype(bf16)

    core_rows = 2 * item_ways * chips * item_share
    id_args = (obs_user, obs_item, obs_count)
    core_send, core_keep, vbuf, gbuf, hbuf, count = call(
        items,
        "item_tiles",
        (
            shape((core_rows, rank), bf16),
            shape((core_rows, rank), f32),
            shape((peers, 2, shard_rows, rank), bf16),
            shape((slots, tile, tile), bf16),
            shape((slots, tile, tile), bf16),
            shape((pairs, rank), f32),
        ),
        [HBM, HBM, HBM] + [VM] * (6 + 2 * peers),
        (*in_hbm(id_args), user_pred, user_imp, own_count, itile, iacc, weights, *received[::-1], *swapped[::-1]),
        (4 * slots * 2 * tile**3, 4000000, 2 * slots * tile * tile),
        tuple(pltpu.SMEM(x.shape, x.dtype) for x in id_args)
        + (pltpu.SemaphoreType.DMA((3,)), pltpu.VMEM((2, item_ways * shard_rows, rank), f32)),
    )

    def users(ou_hbm, oi_hbm, utile_ref, uacc_in, count_ref, vbuf, gbuf, hbuf, *refs):
        outs = refs[: peers + 1]
        ou_ref, oi_ref, sems, uacc = refs[peers + 1 :]
        copies = [
            pltpu.make_async_copy(ou_hbm, ou_ref, sems.at[0]),
            pltpu.make_async_copy(oi_hbm, oi_ref, sems.at[1]),
        ]
        for c in copies:
            c.start()
        pos = lax.axis_index("item")
        count = count_ref[...]
        for u in range(user_blocks):
            total = uacc_in[0, u * tile : (u + 1) * tile]
            for b in range(item_blocks):
                t = u * item_blocks + b
                total = total + utile_ref[t] * count[t : t + 1]
            uacc[0, u * tile : (u + 1) * tile] = total
        uacc[1] = uacc_in[1]
        for c in copies:
            c.wait()
        for k in range(peers):
            group = lax.bitwise_xor(pos, k + 1)
            for s in range(obs_slots):
                at = group * obs_slots + s
                t = k * obs_slots + s
                urows = pl.ds(pl.multiple_of(ou_ref[at] * tile, tile), tile)
                brows = pl.ds(pl.multiple_of(oi_ref[at] * tile, tile), tile)
                uacc[0, urows] += plain(gbuf[t], vbuf[k, 0, brows])
                uacc[1, urows] += plain(hbuf[t], vbuf[k, 1, brows])
        for k in range(item_ways):
            rows = pl.ds(pl.multiple_of(lax.bitwise_xor(pos, k) * share, share), share)
            for m in range(2):
                part = uacc[m, rows]
                if k == 0:
                    outs[peers][m * share : (m + 1) * share] = part
                else:
                    outs[k - 1][m * share : (m + 1) * share] = part.astype(bf16)

    results = call(
        users,
        "user_tiles",
        tuple(shape((2 * share, rank), bf16) for _ in range(peers)) + (shape((2 * share, rank), f32),),
        [HBM, HBM] + [VM] * 6,
        (*in_hbm(id_args[:2]), utile, uacc, count, vbuf, gbuf, hbuf),
        (2 * slots * 2 * tile**3, 4000000, 0),
        tuple(pltpu.SMEM(x.shape, x.dtype) for x in id_args[:2])
        + (pltpu.SemaphoreType.DMA((2,)), pltpu.VMEM((2, user_rows, rank), f32)),
    )
    user_own = results[peers]
    core_recv = core_peer(core_send)
    user_recv = [item_peer(results[k], k + 1) for k in reversed(range(1, peers))]

    chip_rows = 2 * item_ways * item_share

    def fold_core(keep_ref, recv_ref, after_ref, *outs):
        for k in range(chips):
            rows = pl.ds(k * chip_rows, chip_rows)
            outs[k][...] = (keep_ref[rows] + recv_ref[rows].astype(f32)).astype(outs[k].dtype)

    folded = call(
        fold_core,
        "fold_core",
        (shape((chip_rows, rank), f32),) + tuple(shape((chip_rows, rank), bf16) for _ in range(chips - 1)),
        [VM, VM, VM],
        (core_keep, core_recv, user_own),
        (0, 1000, 0),
    )
    chip_recv = [chip_peer(folded[k], k) for k in reversed(range(1, chips))]

    def fold_chips(own_ref, *refs):
        recv = refs[: chips - 1]
        outs = refs[chips - 1 :]
        for k in range(item_ways):
            rows = pl.ds(k * 2 * item_share, 2 * item_share)
            part = own_ref[rows]
            for r in recv:
                part = part + r[rows].astype(f32)
            outs[k][...] = part.astype(outs[k].dtype)

    shares = call(
        fold_chips,
        "fold_chips",
        (shape((2 * item_share, rank), f32),) + tuple(shape((2 * item_share, rank), bf16) for _ in range(peers)),
        [VM] * chips,
        (folded[0], *chip_recv),
        (400000000, 1000, 0),
    )
    near_recv = item_peer(results[0], 1)
    item_recv = [item_peer(shares[k], k) for k in reversed(range(1, item_ways))]

    def sum_users(own_ref, *refs):
        part = own_ref[...]
        for r in refs[:-1]:
            part = part + r[...].astype(f32)
        refs[-1][...] = part

    (user_sum,) = call(
        sum_users,
        "sum_users",
        (shape((2 * share, rank), f32),),
        [VM] * peers,
        (user_own, *user_recv),
        (1200000000, 1000, 0),
    )

    def finish(user_ref, item_ref, *refs):
        near, irecv, outs = refs[0], refs[1 : peers + 1], refs[peers + 1 :]
        for m in range(2):
            rows = pl.ds(m * share, share)
            outs[m][...] = user_ref[rows] + near[rows].astype(f32)
            rows = pl.ds(m * item_share, item_share)
            part = item_ref[rows]
            for r in irecv:
                part = part + r[rows].astype(f32)
            outs[2 + m][...] = part

    return call(
        finish,
        "finish",
        (shape((share, rank), f32),) * 2 + (shape((item_share, rank), f32),) * 2,
        [VM] * (3 + peers),
        (user_sum, shares[0], near_recv, *item_recv),
        (0, 1000, 0),
    )


def solution(mesh):
    in_specs = (
        P("user", None),
        P("user", None),
        P("item", None),
        P("item", None),
        P("user", "item", None),
        P("user", "item", None),
        P("user", "item", None),
        P("user", "item", None),
        P("user", "item", None),
        P("user", "item", None, None, None),
        P("user", "item", None, None, None),
    )
    out_specs = (
        P(("user", "item"), None),
        P(("user", "item"), None),
        P(("item", "user"), None),
        P(("item", "user"), None),
    )
    return jax.shard_map(shards, mesh=mesh, in_specs=in_specs, out_specs=out_specs, check_vma=False)
```

```python
import jax
import jax.numpy as jnp
from jax import lax
from jax.experimental import pallas as pl
from jax.experimental.pallas import tpu as pltpu
from jax.sharding import PartitionSpec as P

loss_weight = 0.015625
cores = 2
vmem_bytes = 16 * 1024 * 1024

VM = pl.BlockSpec(memory_space=pltpu.VMEM)
SM = pl.BlockSpec(memory_space=pltpu.SMEM)
HBM = pl.BlockSpec(memory_space=pltpu.HBM)


def dot(first, second, dims):
    return lax.dot_general(first, second, (dims, ((), ())), preferred_element_type=jnp.float32)


def rows_by_cols(first, second):
    return dot(first, second, ((1,), (1,)))


def plain(first, second):
    return dot(first, second, ((1,), (0,)))


def over_rows(first, second):
    return dot(first, second, ((0,), (0,)))


def call(body, name, out_shapes, specs, args, cost, scratch=()):
    return pl.pallas_call(
        body,
        out_shape=out_shapes,
        in_specs=specs,
        out_specs=tuple(VM for _ in out_shapes),
        scratch_shapes=list(scratch),
        compiler_params=pltpu.CompilerParams(vmem_limit_bytes=vmem_bytes),
        cost_estimate=pl.CostEstimate(flops=cost[0], bytes_accessed=cost[1], transcendentals=cost[2]),
        name=name,
    )(*args)


def in_hbm(arrays):
    return tuple(pltpu.with_memory_space_constraint(x, pltpu.HBM) for x in arrays)


def shape(dims, kind):
    return jax.ShapeDtypeStruct(dims, kind)


def shards(
    user_pred,
    user_imp,
    item_pred,
    item_imp,
    uno_user,
    uno_item,
    obs_user,
    obs_item,
    obs_count,
    obs_label,
    obs_prop,
):
    item_ways = lax.axis_size("item")
    user_ways = lax.axis_size("user")
    chips = user_ways // cores
    tile = obs_label.shape[-1]
    rank = user_pred.shape[1]
    user_rows = user_pred.shape[0]
    shard_rows = item_pred.shape[0]
    user_blocks = user_rows // tile
    item_blocks = shard_rows // tile
    pairs = user_blocks * item_blocks
    half = shard_rows // cores
    share = user_rows // item_ways
    item_share = shard_rows // user_ways
    uno_slots = uno_user.shape[-1] // item_ways
    obs_all = obs_user.shape[-1]
    obs_slots = obs_all // item_ways
    peers = item_ways - 1
    f32 = jnp.float32
    bf16 = jnp.bfloat16

    uno_user = uno_user.reshape(-1)
    uno_item = uno_item.reshape(-1)
    obs_user = obs_user.reshape(-1)
    obs_item = obs_item.reshape(-1)
    obs_count = obs_count.reshape(-1)
    labels = obs_label.reshape(obs_all, tile, tile)
    propens = obs_prop.reshape(obs_all, tile, tile)

    def item_peer(x, k):
        return lax.ppermute(x, "item", [(i, i ^ k) for i in range(item_ways)])

    def core_peer(x):
        return lax.ppermute(x, "user", [(i, i ^ 1) for i in range(user_ways)])

    def chip_peer(x, k):
        return lax.ppermute(x, "user", [(i, i ^ (cores * k)) for i in range(user_ways)])

    def pack(uu_hbm, ui_hbm, vp_hbm, vi_hbm, *refs):
        outs = refs[: peers + 1]
        uu_ref, ui_ref, sems, ssem = refs[peers + 1 :]
        pos = lax.axis_index("item")
        core = lax.rem(lax.axis_index("user"), cores)
        start = pl.multiple_of(core * half, half)
        lists = [
            pltpu.make_async_copy(uu_hbm, uu_ref, ssem.at[0]),
            pltpu.make_async_copy(ui_hbm, ui_ref, ssem.at[1]),
        ]
        for c in lists:
            c.start()
        copies = []
        for k in range(peers):
            for m, ref in enumerate((vp_hbm, vi_hbm)):
                copies.append(
                    pltpu.make_async_copy(
                        ref.at[pl.ds(start, half)], outs[k].at[pl.ds(m * half, half)], sems.at[k, m]
                    )
                )
        for c in copies:
            c.start()
        for c in lists:
            c.wait()
        row = lax.broadcasted_iota(jnp.int32, (pairs, rank), 0)
        for k in range(item_ways):
            group = lax.bitwise_xor(pos, k)
            count = jnp.zeros((pairs, rank), f32)
            for s in range(uno_slots):
                at = group * uno_slots + s
                pair = uu_ref[at] * item_blocks + ui_ref[at]
                count = count + jnp.where(row == pair, 1.0, 0.0)
            if k == 0:
                outs[peers][...] = count
            else:
                outs[k - 1][2 * half :] = count.astype(bf16)
        for c in copies:
            c.wait()

    packed = call(
        pack,
        "pack",
        tuple(shape((2 * half + pairs, rank), bf16) for _ in range(peers)) + (shape((pairs, rank), f32),),
        [HBM, HBM, HBM, HBM],
        in_hbm((uno_user, uno_item, item_pred, item_imp)),
        (0, 400000, 0),
        (
            pltpu.SMEM(uno_user.shape, jnp.int32),
            pltpu.SMEM(uno_item.shape, jnp.int32),
            pltpu.SemaphoreType.DMA((peers, 2)),
            pltpu.SemaphoreType.DMA((2,)),
        ),
    )
    own_count = packed[peers]
    received = [item_peer(packed[k], k + 1) for k in reversed(range(peers))][::-1]

    def observed(logits, imputed, weight, used):
        p = jax.nn.sigmoid(logits)
        q = jax.nn.sigmoid(imputed)
        miss = q - jnp.where(weight < 0, 1.0, 0.0)
        term = jnp.abs(weight) * miss
        g = (((p - q) + term) * (used * loss_weight)).astype(bf16)
        h = (2.0 * term * logits * logits * q * (1.0 - q) * (used * loss_weight)).astype(bf16)
        return g, h

    def local(ou_hbm, oi_hbm, oc_hbm, up_hbm, ux_hbm, vp_hbm, vi_hbm, lab_hbm, prop_hbm, *refs):
        utile_ref, itile_ref, uacc_ref, iacc_ref, w_ref = refs[:5]
        ones = refs[5 : 5 + peers]
        bufs = refs[5 + peers : 14 + peers]
        sems, gbuf, hbuf = refs[14 + peers :]
        ou_ref, oi_ref, oc_ref, up_ref, ux_ref, vp_ref, vi_ref, lab_ref, prop_ref = bufs
        sources = (ou_hbm, oi_hbm, oc_hbm, up_hbm, ux_hbm, vp_hbm, vi_hbm, lab_hbm, prop_hbm)
        copies = [pltpu.make_async_copy(a, b, sems.at[n]) for n, (a, b) in enumerate(zip(sources, bufs))]
        for n in (5, 6, 3, 4, 0, 1, 2, 7, 8):
            copies[n].start()
        pos = lax.axis_index("item")
        for ref in ones:
            ref[...] = jnp.ones_like(ref)
        uacc_ref[...] = jnp.zeros_like(uacc_ref)
        iacc_ref[...] = jnp.zeros_like(iacc_ref)
        for n in (5, 6, 3, 4):
            copies[n].wait()
        for u in range(user_blocks):
            urows = pl.ds(u * tile, tile)
            for b in range(item_blocks):
                irows = pl.ds(b * tile, tile)
                logits = rows_by_cols(up_ref[urows], vp_ref[irows])
                imputed = rows_by_cols(ux_ref[urows], vi_ref[irows])
                gbuf[u * item_blocks + b] = (
                    (jax.nn.sigmoid(logits) - jax.nn.sigmoid(imputed)) * loss_weight
                ).astype(bf16)
        for n in (0, 1, 2, 7, 8):
            copies[n].wait()
        for t in range(obs_all):
            state = lab_ref[t]
            inverse = 1.0 / prop_ref[t].astype(f32)
            w_ref[t] = jnp.where(state == 0, 0.0, jnp.where(state == 2, -inverse, inverse))
        places = []
        for s in range(obs_slots):
            at = pos * obs_slots + s
            urows = pl.ds(pl.multiple_of(ou_ref[at] * tile, tile), tile)
            irows = pl.ds(pl.multiple_of(oi_ref[at] * tile, tile), tile)
            places.append((urows, irows))
            used = jnp.where(s < oc_ref[pos], 1.0, 0.0)
            logits = rows_by_cols(up_ref[urows], vp_ref[irows])
            imputed = rows_by_cols(ux_ref[urows], vi_ref[irows])
            gbuf[pairs + s], hbuf[s] = observed(logits, imputed, w_ref[at], used)
        for u in range(user_blocks):
            urows = pl.ds(u * tile, tile)
            for b in range(item_blocks):
                t = u * item_blocks + b
                utile_ref[t] = plain(gbuf[t], vp_ref[b * tile : (b + 1) * tile])
                itile_ref[t] = over_rows(gbuf[t], up_ref[urows])
        for s, (urows, irows) in enumerate(places):
            uacc_ref[0, urows] += plain(gbuf[pairs + s], vp_ref[irows])
            uacc_ref[1, urows] += plain(hbuf[s], vi_ref[irows])
            iacc_ref[0, irows] += over_rows(gbuf[pairs + s], up_ref[urows])
            iacc_ref[1, irows] += over_rows(hbuf[s], ux_ref[urows])

    local_args = (obs_user, obs_item, obs_count, user_pred, user_imp, item_pred, item_imp, labels, propens)
    utile, itile, uacc, iacc, weights, *ones = call(
        local,
        "local_tiles",
        (
            shape((pairs, tile, rank), f32),
            shape((pairs, tile, rank), f32),
            shape((2, user_rows, rank), f32),
            shape((2, shard_rows, rank), f32),
            shape((obs_all, tile, tile), f32),
            *(shape((16, rank), bf16) for _ in range(peers)),
        ),
        [HBM] * 9,
        in_hbm(local_args),
        (4 * pairs * 2 * tile**3, 8000000, 2 * pairs * tile * tile),
        tuple(pltpu.SMEM(x.shape, x.dtype) for x in local_args[:3])
        + tuple(pltpu.VMEM(x.shape, x.dtype) for x in local_args[3:])
        + (
            pltpu.SemaphoreType.DMA((9,)),
            pltpu.VMEM((pairs + obs_slots, tile, tile), bf16),
            pltpu.VMEM((obs_slots, tile, tile), bf16),
        ),
    )
    swapped = [core_peer(x[: 2 * half] * one[:1]) for x, one in zip(received[::-1], ones)][::-1]

    slots = peers * obs_slots

    near = range(peers)

    def start_ids(sources, targets, sems):
        copies = [pltpu.make_async_copy(a, b, sems.at[n]) for n, (a, b) in enumerate(zip(sources, targets))]
        for c in copies:
            c.start()
        return copies

    def unpack(vbuf, recv, swap):
        core = lax.rem(lax.axis_index("user"), cores)
        mine = pl.multiple_of(core * half, half)
        other = pl.multiple_of((1 - core) * half, half)
        for m in range(2):
            vbuf[m, pl.ds(mine, half)] = recv[m * half : (m + 1) * half]
            vbuf[m, pl.ds(other, half)] = swap[m * half : (m + 1) * half]

    def tiles(k, ou_ref, oi_ref, oc_ref, up_ref, ux_ref, w_ref, vbuf, gbuf, hbuf, first):
        places = []
        group = lax.bitwise_xor(lax.axis_index("item"), k + 1)
        for s in range(obs_slots):
            at = group * obs_slots + s
            urows = pl.ds(pl.multiple_of(ou_ref[at] * tile, tile), tile)
            brows = pl.ds(pl.multiple_of(oi_ref[at] * tile, tile), tile)
            used = jnp.where(s < oc_ref[group], 1.0, 0.0)
            logits = rows_by_cols(up_ref[urows], vbuf[0, brows])
            imputed = rows_by_cols(ux_ref[urows], vbuf[1, brows])
            gbuf[first + s], hbuf[first + s] = observed(logits, imputed, w_ref[at], used)
            places.append((urows, brows, oi_ref[at] * tile, first + s))
        return places

    id_args = (obs_user, obs_item, obs_count)
    id_scratch = tuple(pltpu.SMEM(x.shape, x.dtype) for x in id_args) + (pltpu.SemaphoreType.DMA((3,)),)
    def other_tiles(
        ou_hbm, oi_hbm, oc_hbm, up_ref, ux_ref, count_ref, itile_ref, iacc_in, w_ref, utile_ref, uacc_in, *refs
    ):
        recv = refs[:peers][::-1]
        swap = refs[peers : 2 * peers][::-1]
        send, keep, *outs = refs[2 * peers : 3 * peers + 3]
        ou_ref, oi_ref, oc_ref, sems, vbuf, gbuf, hbuf, iacc, uacc = refs[3 * peers + 3 :]
        copies = start_ids((ou_hbm, oi_hbm, oc_hbm), (ou_ref, oi_ref, oc_ref), sems)
        pos = lax.axis_index("item")
        user = lax.axis_index("user")
        core = lax.rem(user, cores)
        chip = lax.div(user, cores)
        count = count_ref[...]
        for r in recv:
            count = count + r[2 * half :].astype(f32)
        for k in near:
            unpack(vbuf.at[k], recv[k], swap[k])
        iacc[1, :shard_rows] = iacc_in[1]
        for b in range(item_blocks):
            rows = pl.ds(b * tile, tile)
            total = iacc_in[0, rows]
            for u in range(user_blocks):
                t = u * item_blocks + b
                total = total + itile_ref[t] * count[t : t + 1]
            iacc[0, rows] = total
        for u in range(user_blocks):
            rows = pl.ds(u * tile, tile)
            total = uacc_in[0, rows]
            for b in range(item_blocks):
                t = u * item_blocks + b
                total = total + utile_ref[t] * count[t : t + 1]
            uacc[0, rows] = total
        uacc[1] = uacc_in[1]
        for m in range(2):
            iacc[m, shard_rows:] = jnp.zeros((peers * shard_rows, rank), f32)
        for c in copies:
            c.wait()
        places = []
        for k in near:
            for p in tiles(k, ou_ref, oi_ref, oc_ref, up_ref, ux_ref, w_ref, vbuf.at[k], gbuf, hbuf, k * obs_slots):
                places.append((k, p))
        for k, (urows, _, block, t) in places:
            irows = pl.ds(pl.multiple_of((k + 1) * shard_rows + block, tile), tile)
            iacc[0, irows] += over_rows(gbuf[t], up_ref[urows])
            iacc[1, irows] += over_rows(hbuf[t], ux_ref[urows])
        for k, (urows, brows, _, t) in places:
            uacc[0, urows] += plain(gbuf[t], vbuf[k, 0, brows])
            uacc[1, urows] += plain(hbuf[t], vbuf[k, 1, brows])
        for q in range(chips):
            for r in range(item_ways):
                for m in range(2):
                    at = ((q * item_ways + r) * 2 + m) * item_share
                    base = r * shard_rows + lax.bitwise_xor(chip, q) * cores * item_share
                    to_keep = pl.ds(pl.multiple_of(base + core * item_share, item_share), item_share)
                    to_send = pl.ds(pl.multiple_of(base + (1 - core) * item_share, item_share), item_share)
                    keep[at : at + item_share] = iacc[m, to_keep]
                    send[at : at + item_share] = iacc[m, to_send]
        for k in range(item_ways):
            rows = pl.ds(pl.multiple_of(lax.bitwise_xor(pos, k) * share, share), share)
            for m in range(2):
                part = uacc[m, rows]
                if k == 0:
                    outs[peers][m * share : (m + 1) * share] = part
                else:
                    outs[k - 1][m * share : (m + 1) * share] = part.astype(bf16)

    core_rows = 2 * item_ways * chips * item_share
    core_send, core_keep, *results = call(
        other_tiles,
        "other_tiles",
        (shape((core_rows, rank), f32),) * 2
        + tuple(shape((2 * share, rank), bf16) for _ in range(peers))
        + (shape((2 * share, rank), f32),),
        [HBM, HBM, HBM] + [VM] * (8 + 2 * peers),
        (
            *in_hbm(id_args), user_pred, user_imp, own_count, itile, iacc, weights, utile, uacc,
            *received[::-1], *swapped[::-1],
        ),
        (6 * slots * 2 * tile**3, 4000000, 2 * slots * tile * tile),
        id_scratch
        + (
            pltpu.VMEM((peers, 2, shard_rows, rank), bf16),
            pltpu.VMEM((slots, tile, tile), bf16),
            pltpu.VMEM((slots, tile, tile), bf16),
            pltpu.VMEM((2, item_ways * shard_rows, rank), f32),
            pltpu.VMEM((2, user_rows, rank), f32),
        ),
    )
    user_own = results[peers]
    core_recv = core_peer(core_send)
    user_recv = [item_peer(results[k], k + 1) for k in reversed(range(1, peers))]

    chip_rows = 2 * item_ways * item_share

    def fold_core(keep_ref, recv_ref, *outs):
        for k in range(chips):
            rows = pl.ds(k * chip_rows, chip_rows)
            outs[k][...] = (keep_ref[rows] + recv_ref[rows]).astype(outs[k].dtype)

    folded = call(
        fold_core,
        "fold_core",
        (shape((chip_rows, rank), f32),) + tuple(shape((chip_rows, rank), bf16) for _ in range(chips - 1)),
        [VM, VM],
        (core_keep, core_recv),
        (0, 1000, 0),
    )
    chip_recv = [chip_peer(folded[k], k) for k in reversed(range(1, chips))]

    def fold_chips(own_ref, *refs):
        recv = refs[: chips - 1]
        outs = refs[chips - 1 :]
        for k in range(item_ways):
            rows = pl.ds(k * 2 * item_share, 2 * item_share)
            part = own_ref[rows]
            for r in recv:
                part = part + r[rows].astype(f32)
            outs[k][...] = part.astype(outs[k].dtype)

    shares = call(
        fold_chips,
        "fold_chips",
        (shape((2 * item_share, rank), f32),) + tuple(shape((2 * item_share, rank), bf16) for _ in range(peers)),
        [VM] * chips,
        (folded[0], *chip_recv),
        (400000000, 1000, 0),
    )
    near_recv = item_peer(results[0], 1)
    item_recv = [item_peer(shares[k], k) for k in reversed(range(1, item_ways))]

    def sum_users(own_ref, *refs):
        part = own_ref[...]
        for r in refs[:-1]:
            part = part + r[...].astype(f32)
        refs[-1][...] = part

    (user_sum,) = call(
        sum_users,
        "sum_users",
        (shape((2 * share, rank), f32),),
        [VM] * peers,
        (user_own, *user_recv),
        (1200000000, 1000, 0),
    )

    def finish(user_ref, item_ref, *refs):
        near, irecv, outs = refs[0], refs[1 : peers + 1], refs[peers + 1 :]
        for m in range(2):
            rows = pl.ds(m * share, share)
            outs[m][...] = user_ref[rows] + near[rows].astype(f32)
            rows = pl.ds(m * item_share, item_share)
            part = item_ref[rows]
            for r in irecv:
                part = part + r[rows].astype(f32)
            outs[2 + m][...] = part

    return call(
        finish,
        "finish",
        (shape((share, rank), f32),) * 2 + (shape((item_share, rank), f32),) * 2,
        [VM] * (3 + peers),
        (user_sum, shares[0], near_recv, *item_recv),
        (0, 1000, 0),
    )


def solution(mesh):
    in_specs = (
        P("user", None),
        P("user", None),
        P("item", None),
        P("item", None),
        P("user", "item", None),
        P("user", "item", None),
        P("user", "item", None),
        P("user", "item", None),
        P("user", "item", None),
        P("user", "item", None, None, None),
        P("user", "item", None, None, None),
    )
    out_specs = (
        P(("user", "item"), None),
        P(("user", "item"), None),
        P(("item", "user"), None),
        P(("item", "user"), None),
    )
    return jax.shard_map(shards, mesh=mesh, in_specs=in_specs, out_specs=out_specs, check_vma=False)
```

```python
import jax
import jax.numpy as jnp
from jax import lax
from jax.experimental import pallas as pl
from jax.experimental.pallas import tpu as pltpu
from jax.sharding import PartitionSpec as P

loss_weight = 0.015625
cores = 2
vmem_bytes = 16 * 1024 * 1024

VM = pl.BlockSpec(memory_space=pltpu.VMEM)
SM = pl.BlockSpec(memory_space=pltpu.SMEM)
HBM = pl.BlockSpec(memory_space=pltpu.HBM)


def dot(first, second, dims):
    return lax.dot_general(first, second, (dims, ((), ())), preferred_element_type=jnp.float32)


def rows_by_cols(first, second):
    return dot(first, second, ((1,), (1,)))


def plain(first, second):
    return dot(first, second, ((1,), (0,)))


def over_rows(first, second):
    return dot(first, second, ((0,), (0,)))


def call(body, name, out_shapes, specs, args, cost, scratch=()):
    return pl.pallas_call(
        body,
        out_shape=out_shapes,
        in_specs=specs,
        out_specs=tuple(VM for _ in out_shapes),
        scratch_shapes=list(scratch),
        compiler_params=pltpu.CompilerParams(vmem_limit_bytes=vmem_bytes),
        cost_estimate=pl.CostEstimate(flops=cost[0], bytes_accessed=cost[1], transcendentals=cost[2]),
        name=name,
    )(*args)


def in_hbm(arrays):
    return tuple(pltpu.with_memory_space_constraint(x, pltpu.HBM) for x in arrays)


def shape(dims, kind):
    return jax.ShapeDtypeStruct(dims, kind)


def shards(
    user_pred,
    user_imp,
    item_pred,
    item_imp,
    uno_user,
    uno_item,
    obs_user,
    obs_item,
    obs_count,
    obs_label,
    obs_prop,
):
    item_ways = lax.axis_size("item")
    user_ways = lax.axis_size("user")
    chips = user_ways // cores
    tile = obs_label.shape[-1]
    rank = user_pred.shape[1]
    user_rows = user_pred.shape[0]
    shard_rows = item_pred.shape[0]
    user_blocks = user_rows // tile
    item_blocks = shard_rows // tile
    pairs = user_blocks * item_blocks
    half = shard_rows // cores
    share = user_rows // item_ways
    item_share = shard_rows // user_ways
    uno_slots = uno_user.shape[-1] // item_ways
    obs_all = obs_user.shape[-1]
    obs_slots = obs_all // item_ways
    peers = item_ways - 1
    f32 = jnp.float32
    bf16 = jnp.bfloat16

    uno_user = uno_user.reshape(-1)
    uno_item = uno_item.reshape(-1)
    obs_user = obs_user.reshape(-1)
    obs_item = obs_item.reshape(-1)
    obs_count = obs_count.reshape(-1)
    labels = obs_label.reshape(obs_all, tile, tile)
    propens = obs_prop.reshape(obs_all, tile, tile)

    def item_peer(x, k):
        return lax.ppermute(x, "item", [(i, i ^ k) for i in range(item_ways)])

    def core_peer(x):
        return lax.ppermute(x, "user", [(i, i ^ 1) for i in range(user_ways)])

    def chip_peer(x, k):
        return lax.ppermute(x, "user", [(i, i ^ (cores * k)) for i in range(user_ways)])

    def pack(uu_hbm, ui_hbm, vp_hbm, vi_hbm, *refs):
        outs = refs[: peers + 1]
        uu_ref, ui_ref, sems, ssem = refs[peers + 1 :]
        pos = lax.axis_index("item")
        core = lax.rem(lax.axis_index("user"), cores)
        start = pl.multiple_of(core * half, half)
        lists = [
            pltpu.make_async_copy(uu_hbm, uu_ref, ssem.at[0]),
            pltpu.make_async_copy(ui_hbm, ui_ref, ssem.at[1]),
        ]
        for c in lists:
            c.start()
        copies = []
        for k in range(peers):
            for m, ref in enumerate((vp_hbm, vi_hbm)):
                copies.append(
                    pltpu.make_async_copy(
                        ref.at[pl.ds(start, half)], outs[k].at[pl.ds(m * half, half)], sems.at[k, m]
                    )
                )
        for c in copies:
            c.start()
        for c in lists:
            c.wait()
        row = lax.broadcasted_iota(jnp.int32, (pairs, rank), 0)
        for k in range(item_ways):
            group = lax.bitwise_xor(pos, k)
            count = jnp.zeros((pairs, rank), f32)
            for s in range(uno_slots):
                at = group * uno_slots + s
                pair = uu_ref[at] * item_blocks + ui_ref[at]
                count = count + jnp.where(row == pair, 1.0, 0.0)
            if k == 0:
                outs[peers][...] = count
            else:
                outs[k - 1][2 * half :] = count.astype(bf16)
        for c in copies:
            c.wait()

    packed = call(
        pack,
        "pack",
        tuple(shape((2 * half + pairs, rank), bf16) for _ in range(peers)) + (shape((pairs, rank), f32),),
        [HBM, HBM, HBM, HBM],
        in_hbm((uno_user, uno_item, item_pred, item_imp)),
        (0, 400000, 0),
        (
            pltpu.SMEM(uno_user.shape, jnp.int32),
            pltpu.SMEM(uno_item.shape, jnp.int32),
            pltpu.SemaphoreType.DMA((peers, 2)),
            pltpu.SemaphoreType.DMA((2,)),
        ),
    )
    own_count = packed[peers]
    received = [item_peer(packed[k], k + 1) for k in reversed(range(peers))][::-1]

    def observed(logits, imputed, weight, used):
        p = jax.nn.sigmoid(logits)
        q = jax.nn.sigmoid(imputed)
        miss = q - jnp.where(weight < 0, 1.0, 0.0)
        term = jnp.abs(weight) * miss
        g = (((p - q) + term) * (used * loss_weight)).astype(bf16)
        h = (2.0 * term * logits * logits * q * (1.0 - q) * (used * loss_weight)).astype(bf16)
        return g, h

    def local(ou_hbm, oi_hbm, oc_hbm, up_hbm, ux_hbm, vp_hbm, vi_hbm, lab_hbm, prop_hbm, *refs):
        utile_ref, itile_ref, uacc_ref, iacc_ref, w_ref = refs[:5]
        ones = refs[5 : 5 + peers]
        bufs = refs[5 + peers : 14 + peers]
        sems, gbuf, hbuf = refs[14 + peers :]
        ou_ref, oi_ref, oc_ref, up_ref, ux_ref, vp_ref, vi_ref, lab_ref, prop_ref = bufs
        sources = (ou_hbm, oi_hbm, oc_hbm, up_hbm, ux_hbm, vp_hbm, vi_hbm, lab_hbm, prop_hbm)
        copies = [pltpu.make_async_copy(a, b, sems.at[n]) for n, (a, b) in enumerate(zip(sources, bufs))]
        for n in (5, 6, 3, 4, 0, 1, 2, 7, 8):
            copies[n].start()
        pos = lax.axis_index("item")
        for ref in ones:
            ref[...] = jnp.ones_like(ref)
        uacc_ref[...] = jnp.zeros_like(uacc_ref)
        iacc_ref[...] = jnp.zeros_like(iacc_ref)
        for n in (5, 6, 3, 4):
            copies[n].wait()
        for u in range(user_blocks):
            urows = pl.ds(u * tile, tile)
            for b in range(item_blocks):
                irows = pl.ds(b * tile, tile)
                logits = rows_by_cols(up_ref[urows], vp_ref[irows])
                imputed = rows_by_cols(ux_ref[urows], vi_ref[irows])
                gbuf[u * item_blocks + b] = (
                    (jax.nn.sigmoid(logits) - jax.nn.sigmoid(imputed)) * loss_weight
                ).astype(bf16)
        for n in (0, 1, 2, 7, 8):
            copies[n].wait()
        for t in range(obs_all):
            state = lab_ref[t]
            inverse = 1.0 / prop_ref[t].astype(f32)
            w_ref[t] = jnp.where(state == 0, 0.0, jnp.where(state == 2, -inverse, inverse))
        places = []
        for s in range(obs_slots):
            at = pos * obs_slots + s
            urows = pl.ds(pl.multiple_of(ou_ref[at] * tile, tile), tile)
            irows = pl.ds(pl.multiple_of(oi_ref[at] * tile, tile), tile)
            places.append((urows, irows))
            used = jnp.where(s < oc_ref[pos], 1.0, 0.0)
            logits = rows_by_cols(up_ref[urows], vp_ref[irows])
            imputed = rows_by_cols(ux_ref[urows], vi_ref[irows])
            gbuf[pairs + s], hbuf[s] = observed(logits, imputed, w_ref[at], used)
        for u in range(user_blocks):
            urows = pl.ds(u * tile, tile)
            for b in range(item_blocks):
                t = u * item_blocks + b
                utile_ref[t] = plain(gbuf[t], vp_ref[b * tile : (b + 1) * tile])
                itile_ref[t] = over_rows(gbuf[t], up_ref[urows])
        for s, (urows, irows) in enumerate(places):
            uacc_ref[0, urows] += plain(gbuf[pairs + s], vp_ref[irows])
            uacc_ref[1, urows] += plain(hbuf[s], vi_ref[irows])
            iacc_ref[0, irows] += over_rows(gbuf[pairs + s], up_ref[urows])
            iacc_ref[1, irows] += over_rows(hbuf[s], ux_ref[urows])

    local_args = (obs_user, obs_item, obs_count, user_pred, user_imp, item_pred, item_imp, labels, propens)
    utile, itile, uacc, iacc, weights, *ones = call(
        local,
        "local_tiles",
        (
            shape((pairs, tile, rank), f32),
            shape((pairs, tile, rank), f32),
            shape((2, user_rows, rank), f32),
            shape((2, shard_rows, rank), f32),
            shape((obs_all, tile, tile), f32),
            *(shape((16, rank), bf16) for _ in range(peers)),
        ),
        [HBM] * 9,
        in_hbm(local_args),
        (4 * pairs * 2 * tile**3, 8000000, 2 * pairs * tile * tile),
        tuple(pltpu.SMEM(x.shape, x.dtype) for x in local_args[:3])
        + tuple(pltpu.VMEM(x.shape, x.dtype) for x in local_args[3:])
        + (
            pltpu.SemaphoreType.DMA((9,)),
            pltpu.VMEM((pairs + obs_slots, tile, tile), bf16),
            pltpu.VMEM((obs_slots, tile, tile), bf16),
        ),
    )
    swapped = [core_peer(x[: 2 * half] * one[:1]) for x, one in zip(received, ones)]

    slots = peers * obs_slots

    near = range(peers)
    first_order = [peers - 1, *range(peers - 1)]

    def start_ids(sources, targets, sems):
        copies = [pltpu.make_async_copy(a, b, sems.at[n]) for n, (a, b) in enumerate(zip(sources, targets))]
        for c in copies:
            c.start()
        return copies

    def unpack(vbuf, recv, swap):
        core = lax.rem(lax.axis_index("user"), cores)
        mine = pl.multiple_of(core * half, half)
        other = pl.multiple_of((1 - core) * half, half)
        for m in range(2):
            vbuf[m, pl.ds(mine, half)] = recv[m * half : (m + 1) * half]
            vbuf[m, pl.ds(other, half)] = swap[m * half : (m + 1) * half]

    def tiles(k, ou_ref, oi_ref, oc_ref, up_ref, ux_ref, w_ref, vbuf, gbuf, hbuf, first):
        places = []
        group = lax.bitwise_xor(lax.axis_index("item"), k + 1)
        for s in range(obs_slots):
            at = group * obs_slots + s
            urows = pl.ds(pl.multiple_of(ou_ref[at] * tile, tile), tile)
            brows = pl.ds(pl.multiple_of(oi_ref[at] * tile, tile), tile)
            used = jnp.where(s < oc_ref[group], 1.0, 0.0)
            logits = rows_by_cols(up_ref[urows], vbuf[0, brows])
            imputed = rows_by_cols(ux_ref[urows], vbuf[1, brows])
            gbuf[first + s], hbuf[first + s] = observed(logits, imputed, w_ref[at], used)
            places.append((urows, brows, oi_ref[at] * tile, first + s))
        return places

    id_args = (obs_user, obs_item, obs_count)
    id_scratch = tuple(pltpu.SMEM(x.shape, x.dtype) for x in id_args) + (pltpu.SemaphoreType.DMA((3,)),)
    def other_tiles(
        ou_hbm, oi_hbm, oc_hbm, up_ref, ux_ref, count_ref, itile_ref, iacc_in, w_ref, utile_ref, uacc_in, *refs
    ):
        recv = [refs[first_order.index(k)] for k in range(peers)]
        swap = [refs[peers + first_order.index(k)] for k in range(peers)]
        send, keep, *outs = refs[2 * peers : 3 * peers + 3]
        ou_ref, oi_ref, oc_ref, sems, vbuf, gbuf, hbuf, iacc, uacc = refs[3 * peers + 3 :]
        copies = start_ids((ou_hbm, oi_hbm, oc_hbm), (ou_ref, oi_ref, oc_ref), sems)
        pos = lax.axis_index("item")
        user = lax.axis_index("user")
        core = lax.rem(user, cores)
        chip = lax.div(user, cores)
        count = count_ref[...]
        for r in recv:
            count = count + r[2 * half :].astype(f32)
        for k in near:
            unpack(vbuf.at[k], recv[k], swap[k])
        iacc[1, :shard_rows] = iacc_in[1]
        for b in range(item_blocks):
            rows = pl.ds(b * tile, tile)
            total = iacc_in[0, rows]
            for u in range(user_blocks):
                t = u * item_blocks + b
                total = total + itile_ref[t] * count[t : t + 1]
            iacc[0, rows] = total
        for u in range(user_blocks):
            rows = pl.ds(u * tile, tile)
            total = uacc_in[0, rows]
            for b in range(item_blocks):
                t = u * item_blocks + b
                total = total + utile_ref[t] * count[t : t + 1]
            uacc[0, rows] = total
        uacc[1] = uacc_in[1]
        for m in range(2):
            iacc[m, shard_rows:] = jnp.zeros((peers * shard_rows, rank), f32)
        for c in copies:
            c.wait()
        places = []
        for k in near:
            for p in tiles(k, ou_ref, oi_ref, oc_ref, up_ref, ux_ref, w_ref, vbuf.at[k], gbuf, hbuf, k * obs_slots):
                places.append((k, p))
        for k, (urows, _, block, t) in places:
            irows = pl.ds(pl.multiple_of((k + 1) * shard_rows + block, tile), tile)
            iacc[0, irows] += over_rows(gbuf[t], up_ref[urows])
            iacc[1, irows] += over_rows(hbuf[t], ux_ref[urows])
        for k, (urows, brows, _, t) in places:
            uacc[0, urows] += plain(gbuf[t], vbuf[k, 0, brows])
            uacc[1, urows] += plain(hbuf[t], vbuf[k, 1, brows])
        for q in range(chips):
            for r in range(item_ways):
                for m in range(2):
                    at = ((q * item_ways + r) * 2 + m) * item_share
                    base = r * shard_rows + lax.bitwise_xor(chip, q) * cores * item_share
                    to_keep = pl.ds(pl.multiple_of(base + core * item_share, item_share), item_share)
                    to_send = pl.ds(pl.multiple_of(base + (1 - core) * item_share, item_share), item_share)
                    keep[at : at + item_share] = iacc[m, to_keep]
                    send[at : at + item_share] = iacc[m, to_send]
        for k in range(item_ways):
            rows = pl.ds(pl.multiple_of(lax.bitwise_xor(pos, k) * share, share), share)
            for m in range(2):
                part = uacc[m, rows]
                if k == 0:
                    outs[peers][m * share : (m + 1) * share] = part
                else:
                    outs[k - 1][m * share : (m + 1) * share] = part.astype(bf16)

    core_rows = 2 * item_ways * chips * item_share
    core_send, core_keep, *results = call(
        other_tiles,
        "other_tiles",
        (shape((core_rows, rank), f32),) * 2
        + tuple(shape((2 * share, rank), bf16) for _ in range(peers))
        + (shape((2 * share, rank), f32),),
        [HBM, HBM, HBM] + [VM] * (8 + 2 * peers),
        (
            *in_hbm(id_args), user_pred, user_imp, own_count, itile, iacc, weights, utile, uacc,
            *(received[k] for k in first_order), *(swapped[k] for k in first_order),
        ),
        (6 * slots * 2 * tile**3, 4000000, 2 * slots * tile * tile),
        id_scratch
        + (
            pltpu.VMEM((peers, 2, shard_rows, rank), bf16),
            pltpu.VMEM((slots, tile, tile), bf16),
            pltpu.VMEM((slots, tile, tile), bf16),
            pltpu.VMEM((2, item_ways * shard_rows, rank), f32),
            pltpu.VMEM((2, user_rows, rank), f32),
        ),
    )
    user_own = results[peers]
    core_recv = core_peer(core_send)
    user_recv = [item_peer(results[k], k + 1) for k in reversed(range(1, peers))]

    chip_rows = 2 * item_ways * item_share

    def fold_core(keep_ref, recv_ref, *outs):
        for k in range(chips):
            rows = pl.ds(k * chip_rows, chip_rows)
            outs[k][...] = (keep_ref[rows] + recv_ref[rows]).astype(outs[k].dtype)

    folded = call(
        fold_core,
        "fold_core",
        (shape((chip_rows, rank), f32),) + tuple(shape((chip_rows, rank), bf16) for _ in range(chips - 1)),
        [VM, VM],
        (core_keep, core_recv),
        (0, 1000, 0),
    )
    chip_recv = [chip_peer(folded[k], k) for k in reversed(range(1, chips))]

    def fold_chips(own_ref, *refs):
        recv = refs[: chips - 1]
        outs = refs[chips - 1 :]
        for k in range(item_ways):
            rows = pl.ds(k * 2 * item_share, 2 * item_share)
            part = own_ref[rows]
            for r in recv:
                part = part + r[rows].astype(f32)
            outs[k][...] = part.astype(outs[k].dtype)

    shares = call(
        fold_chips,
        "fold_chips",
        (shape((2 * item_share, rank), f32),) + tuple(shape((2 * item_share, rank), bf16) for _ in range(peers)),
        [VM] * chips,
        (folded[0], *chip_recv),
        (400000000, 1000, 0),
    )
    near_recv = item_peer(results[0], 1)
    item_recv = [item_peer(shares[k], k) for k in reversed(range(1, item_ways))]

    def sum_users(own_ref, *refs):
        part = own_ref[...]
        for r in refs[:-1]:
            part = part + r[...].astype(f32)
        refs[-1][...] = part

    (user_sum,) = call(
        sum_users,
        "sum_users",
        (shape((2 * share, rank), f32),),
        [VM] * peers,
        (user_own, *user_recv),
        (1200000000, 1000, 0),
    )

    def finish(user_ref, item_ref, *refs):
        near, irecv, outs = refs[0], refs[1 : peers + 1], refs[peers + 1 :]
        for m in range(2):
            rows = pl.ds(m * share, share)
            outs[m][...] = user_ref[rows] + near[rows].astype(f32)
            rows = pl.ds(m * item_share, item_share)
            part = item_ref[rows]
            for r in irecv:
                part = part + r[rows].astype(f32)
            outs[2 + m][...] = part

    return call(
        finish,
        "finish",
        (shape((share, rank), f32),) * 2 + (shape((item_share, rank), f32),) * 2,
        [VM] * (3 + peers),
        (user_sum, shares[0], near_recv, *item_recv),
        (0, 1000, 0),
    )


def solution(mesh):
    in_specs = (
        P("user", None),
        P("user", None),
        P("item", None),
        P("item", None),
        P("user", "item", None),
        P("user", "item", None),
        P("user", "item", None),
        P("user", "item", None),
        P("user", "item", None),
        P("user", "item", None, None, None),
        P("user", "item", None, None, None),
    )
    out_specs = (
        P(("user", "item"), None),
        P(("user", "item"), None),
        P(("item", "user"), None),
        P(("item", "user"), None),
    )
    return jax.shard_map(shards, mesh=mesh, in_specs=in_specs, out_specs=out_specs, check_vma=False)
```

```python
import jax
import jax.numpy as jnp
from jax import lax
from jax.experimental import pallas as pl
from jax.experimental.pallas import tpu as pltpu
from jax.sharding import PartitionSpec as P

loss_weight = 0.015625
cores = 2
vmem_bytes = 16 * 1024 * 1024

VM = pl.BlockSpec(memory_space=pltpu.VMEM)
SM = pl.BlockSpec(memory_space=pltpu.SMEM)
HBM = pl.BlockSpec(memory_space=pltpu.HBM)


def dot(first, second, dims):
    return lax.dot_general(first, second, (dims, ((), ())), preferred_element_type=jnp.float32)


def rows_by_cols(first, second):
    return dot(first, second, ((1,), (1,)))


def plain(first, second):
    return dot(first, second, ((1,), (0,)))


def over_rows(first, second):
    return dot(first, second, ((0,), (0,)))


def call(body, name, out_shapes, specs, args, cost, scratch=()):
    return pl.pallas_call(
        body,
        out_shape=out_shapes,
        in_specs=specs,
        out_specs=tuple(VM for _ in out_shapes),
        scratch_shapes=list(scratch),
        compiler_params=pltpu.CompilerParams(vmem_limit_bytes=vmem_bytes),
        cost_estimate=pl.CostEstimate(flops=cost[0], bytes_accessed=cost[1], transcendentals=cost[2]),
        name=name,
    )(*args)


def in_hbm(arrays):
    return tuple(pltpu.with_memory_space_constraint(x, pltpu.HBM) for x in arrays)


def shape(dims, kind):
    return jax.ShapeDtypeStruct(dims, kind)


def shards(
    user_pred,
    user_imp,
    item_pred,
    item_imp,
    uno_user,
    uno_item,
    obs_user,
    obs_item,
    obs_count,
    obs_label,
    obs_prop,
):
    item_ways = lax.axis_size("item")
    user_ways = lax.axis_size("user")
    chips = user_ways // cores
    tile = obs_label.shape[-1]
    rank = user_pred.shape[1]
    user_rows = user_pred.shape[0]
    shard_rows = item_pred.shape[0]
    user_blocks = user_rows // tile
    item_blocks = shard_rows // tile
    pairs = user_blocks * item_blocks
    half = shard_rows // cores
    share = user_rows // item_ways
    item_share = shard_rows // user_ways
    uno_slots = uno_user.shape[-1] // item_ways
    obs_all = obs_user.shape[-1]
    obs_slots = obs_all // item_ways
    peers = item_ways - 1
    f32 = jnp.float32
    bf16 = jnp.bfloat16

    uno_user = uno_user.reshape(-1)
    uno_item = uno_item.reshape(-1)
    obs_user = obs_user.reshape(-1)
    obs_item = obs_item.reshape(-1)
    obs_count = obs_count.reshape(-1)
    labels = obs_label.reshape(obs_all, tile, tile)
    propens = obs_prop.reshape(obs_all, tile, tile)

    def item_peer(x, k):
        return lax.ppermute(x, "item", [(i, i ^ k) for i in range(item_ways)])

    def core_peer(x):
        return lax.ppermute(x, "user", [(i, i ^ 1) for i in range(user_ways)])

    def chip_peer(x, k):
        return lax.ppermute(x, "user", [(i, i ^ (cores * k)) for i in range(user_ways)])

    def pack(uu_hbm, ui_hbm, vp_hbm, vi_hbm, *refs):
        outs = refs[: peers + 1]
        uu_ref, ui_ref, sems, ssem = refs[peers + 1 :]
        pos = lax.axis_index("item")
        core = lax.rem(lax.axis_index("user"), cores)
        start = pl.multiple_of(core * half, half)
        lists = [
            pltpu.make_async_copy(uu_hbm, uu_ref, ssem.at[0]),
            pltpu.make_async_copy(ui_hbm, ui_ref, ssem.at[1]),
        ]
        for c in lists:
            c.start()
        copies = []
        for k in range(peers):
            for m, ref in enumerate((vp_hbm, vi_hbm)):
                copies.append(
                    pltpu.make_async_copy(
                        ref.at[pl.ds(start, half)], outs[k].at[pl.ds(m * half, half)], sems.at[k, m]
                    )
                )
        for c in copies:
            c.start()
        for c in lists:
            c.wait()
        row = lax.broadcasted_iota(jnp.int32, (pairs, rank), 0)
        for k in range(item_ways):
            group = lax.bitwise_xor(pos, k)
            count = jnp.zeros((pairs, rank), f32)
            for s in range(uno_slots):
                at = group * uno_slots + s
                pair = uu_ref[at] * item_blocks + ui_ref[at]
                count = count + jnp.where(row == pair, 1.0, 0.0)
            if k == 0:
                outs[peers][...] = count
            else:
                outs[k - 1][2 * half :] = count.astype(bf16)
        for c in copies:
            c.wait()

    packed = call(
        pack,
        "pack",
        tuple(shape((2 * half + pairs, rank), bf16) for _ in range(peers)) + (shape((pairs, rank), f32),),
        [HBM, HBM, HBM, HBM],
        in_hbm((uno_user, uno_item, item_pred, item_imp)),
        (0, 400000, 0),
        (
            pltpu.SMEM(uno_user.shape, jnp.int32),
            pltpu.SMEM(uno_item.shape, jnp.int32),
            pltpu.SemaphoreType.DMA((peers, 2)),
            pltpu.SemaphoreType.DMA((2,)),
        ),
    )
    own_count = packed[peers]
    received = [item_peer(packed[k], k + 1) for k in reversed(range(peers))][::-1]

    def observed(logits, imputed, weight, used):
        p = jax.nn.sigmoid(logits)
        q = jax.nn.sigmoid(imputed)
        miss = q - jnp.where(weight < 0, 1.0, 0.0)
        term = jnp.abs(weight) * miss
        g = (((p - q) + term) * (used * loss_weight)).astype(bf16)
        h = (2.0 * term * logits * logits * q * (1.0 - q) * (used * loss_weight)).astype(bf16)
        return g, h

    def local(ou_hbm, oi_hbm, oc_hbm, up_hbm, ux_hbm, vp_hbm, vi_hbm, lab_hbm, prop_hbm, *refs):
        utile_ref, itile_ref, uacc_ref, iacc_ref, w_ref = refs[:5]
        ones = refs[5 : 5 + peers]
        bufs = refs[5 + peers : 14 + peers]
        sems, gbuf, hbuf = refs[14 + peers :]
        ou_ref, oi_ref, oc_ref, up_ref, ux_ref, vp_ref, vi_ref, lab_ref, prop_ref = bufs
        sources = (ou_hbm, oi_hbm, oc_hbm, up_hbm, ux_hbm, vp_hbm, vi_hbm, lab_hbm, prop_hbm)
        copies = [pltpu.make_async_copy(a, b, sems.at[n]) for n, (a, b) in enumerate(zip(sources, bufs))]
        for n in (5, 6, 3, 4, 0, 1, 2, 7, 8):
            copies[n].start()
        pos = lax.axis_index("item")
        for ref in ones:
            ref[...] = jnp.ones_like(ref)
        uacc_ref[...] = jnp.zeros_like(uacc_ref)
        iacc_ref[...] = jnp.zeros_like(iacc_ref)
        for n in (5, 6, 3, 4):
            copies[n].wait()
        for u in range(user_blocks):
            urows = pl.ds(u * tile, tile)
            for b in range(item_blocks):
                irows = pl.ds(b * tile, tile)
                logits = rows_by_cols(up_ref[urows], vp_ref[irows])
                imputed = rows_by_cols(ux_ref[urows], vi_ref[irows])
                gbuf[u * item_blocks + b] = (
                    (jax.nn.sigmoid(logits) - jax.nn.sigmoid(imputed)) * loss_weight
                ).astype(bf16)
        for n in (0, 1, 2, 7, 8):
            copies[n].wait()
        for t in range(obs_all):
            state = lab_ref[t]
            inverse = 1.0 / prop_ref[t].astype(f32)
            w_ref[t] = jnp.where(state == 0, 0.0, jnp.where(state == 2, -inverse, inverse))
        places = []
        for s in range(obs_slots):
            at = pos * obs_slots + s
            urows = pl.ds(pl.multiple_of(ou_ref[at] * tile, tile), tile)
            irows = pl.ds(pl.multiple_of(oi_ref[at] * tile, tile), tile)
            places.append((urows, irows))
            used = jnp.where(s < oc_ref[pos], 1.0, 0.0)
            logits = rows_by_cols(up_ref[urows], vp_ref[irows])
            imputed = rows_by_cols(ux_ref[urows], vi_ref[irows])
            gbuf[pairs + s], hbuf[s] = observed(logits, imputed, w_ref[at], used)
        for u in range(user_blocks):
            urows = pl.ds(u * tile, tile)
            for b in range(item_blocks):
                t = u * item_blocks + b
                utile_ref[t] = plain(gbuf[t], vp_ref[b * tile : (b + 1) * tile])
                itile_ref[t] = over_rows(gbuf[t], up_ref[urows])
        for s, (urows, irows) in enumerate(places):
            uacc_ref[0, urows] += plain(gbuf[pairs + s], vp_ref[irows])
            uacc_ref[1, urows] += plain(hbuf[s], vi_ref[irows])
            iacc_ref[0, irows] += over_rows(gbuf[pairs + s], up_ref[urows])
            iacc_ref[1, irows] += over_rows(hbuf[s], ux_ref[urows])

    local_args = (obs_user, obs_item, obs_count, user_pred, user_imp, item_pred, item_imp, labels, propens)
    utile, itile, uacc, iacc, weights, *ones = call(
        local,
        "local_tiles",
        (
            shape((pairs, tile, rank), f32),
            shape((pairs, tile, rank), f32),
            shape((2, user_rows, rank), f32),
            shape((2, shard_rows, rank), f32),
            shape((obs_all, tile, tile), f32),
            *(shape((16, rank), bf16) for _ in range(peers)),
        ),
        [HBM] * 9,
        in_hbm(local_args),
        (4 * pairs * 2 * tile**3, 8000000, 2 * pairs * tile * tile),
        tuple(pltpu.SMEM(x.shape, x.dtype) for x in local_args[:3])
        + tuple(pltpu.VMEM(x.shape, x.dtype) for x in local_args[3:])
        + (
            pltpu.SemaphoreType.DMA((9,)),
            pltpu.VMEM((pairs + obs_slots, tile, tile), bf16),
            pltpu.VMEM((obs_slots, tile, tile), bf16),
        ),
    )
    swapped = [core_peer(x[: 2 * half] * one[:1]) for x, one in zip(received, ones)]

    slots = peers * obs_slots

    near = range(peers)
    first_order = [peers - 1, *range(peers - 1)]

    def start_ids(sources, targets, sems):
        copies = [pltpu.make_async_copy(a, b, sems.at[n]) for n, (a, b) in enumerate(zip(sources, targets))]
        for c in copies:
            c.start()
        return copies

    def unpack(vbuf, recv, swap):
        core = lax.rem(lax.axis_index("user"), cores)
        mine = pl.multiple_of(core * half, half)
        other = pl.multiple_of((1 - core) * half, half)
        for m in range(2):
            vbuf[m, pl.ds(mine, half)] = recv[m * half : (m + 1) * half]
            vbuf[m, pl.ds(other, half)] = swap[m * half : (m + 1) * half]

    def tiles(k, ou_ref, oi_ref, oc_ref, up_ref, ux_ref, w_ref, vbuf, gbuf, hbuf, first):
        places = []
        group = lax.bitwise_xor(lax.axis_index("item"), k + 1)
        for s in range(obs_slots):
            at = group * obs_slots + s
            urows = pl.ds(pl.multiple_of(ou_ref[at] * tile, tile), tile)
            brows = pl.ds(pl.multiple_of(oi_ref[at] * tile, tile), tile)
            used = jnp.where(s < oc_ref[group], 1.0, 0.0)
            logits = rows_by_cols(up_ref[urows], vbuf[0, brows])
            imputed = rows_by_cols(ux_ref[urows], vbuf[1, brows])
            gbuf[first + s], hbuf[first + s] = observed(logits, imputed, w_ref[at], used)
            places.append((urows, brows, oi_ref[at] * tile, first + s))
        return places

    id_args = (obs_user, obs_item, obs_count)
    id_scratch = tuple(pltpu.SMEM(x.shape, x.dtype) for x in id_args) + (pltpu.SemaphoreType.DMA((3,)),)
    def other_tiles(
        ou_hbm, oi_hbm, oc_hbm, up_ref, ux_ref, count_ref, itile_ref, iacc_in, w_ref, utile_ref, uacc_in, *refs
    ):
        recv = [refs[first_order.index(k)] for k in range(peers)]
        swap = [refs[peers + first_order.index(k)] for k in range(peers)]
        send, keep, *outs = refs[2 * peers : 3 * peers + 3]
        ou_ref, oi_ref, oc_ref, sems, vbuf, gbuf, hbuf, iacc, uacc = refs[3 * peers + 3 :]
        copies = start_ids((ou_hbm, oi_hbm, oc_hbm), (ou_ref, oi_ref, oc_ref), sems)
        pos = lax.axis_index("item")
        user = lax.axis_index("user")
        core = lax.rem(user, cores)
        chip = lax.div(user, cores)
        count = count_ref[...]
        for r in recv:
            count = count + r[2 * half :].astype(f32)
        for k in near:
            unpack(vbuf.at[k], recv[k], swap[k])
        iacc[1, :shard_rows] = iacc_in[1]
        for b in range(item_blocks):
            rows = pl.ds(b * tile, tile)
            total = iacc_in[0, rows]
            for u in range(user_blocks):
                t = u * item_blocks + b
                total = total + itile_ref[t] * count[t : t + 1]
            iacc[0, rows] = total
        for u in range(user_blocks):
            rows = pl.ds(u * tile, tile)
            total = uacc_in[0, rows]
            for b in range(item_blocks):
                t = u * item_blocks + b
                total = total + utile_ref[t] * count[t : t + 1]
            uacc[0, rows] = total
        uacc[1] = uacc_in[1]
        for m in range(2):
            iacc[m, shard_rows:] = jnp.zeros((peers * shard_rows, rank), f32)
        for c in copies:
            c.wait()
        places = []
        for k in near:
            for p in tiles(k, ou_ref, oi_ref, oc_ref, up_ref, ux_ref, w_ref, vbuf.at[k], gbuf, hbuf, k * obs_slots):
                places.append((k, p))
        for k, (urows, _, block, t) in places:
            irows = pl.ds(pl.multiple_of((k + 1) * shard_rows + block, tile), tile)
            iacc[0, irows] += over_rows(gbuf[t], up_ref[urows])
            iacc[1, irows] += over_rows(hbuf[t], ux_ref[urows])
        for k, (urows, brows, _, t) in places:
            uacc[0, urows] += plain(gbuf[t], vbuf[k, 0, brows])
            uacc[1, urows] += plain(hbuf[t], vbuf[k, 1, brows])
        for q in range(chips):
            for r in range(item_ways):
                for m in range(2):
                    at = ((q * item_ways + r) * 2 + m) * item_share
                    base = r * shard_rows + lax.bitwise_xor(chip, q) * cores * item_share
                    to_keep = pl.ds(pl.multiple_of(base + core * item_share, item_share), item_share)
                    to_send = pl.ds(pl.multiple_of(base + (1 - core) * item_share, item_share), item_share)
                    keep[at : at + item_share] = iacc[m, to_keep]
                    send[at : at + item_share] = iacc[m, to_send]
        for k in range(item_ways):
            rows = pl.ds(pl.multiple_of(lax.bitwise_xor(pos, k) * share, share), share)
            for m in range(2):
                part = uacc[m, rows]
                if k == 0:
                    outs[peers][m * share : (m + 1) * share] = part
                else:
                    outs[k - 1][m * share : (m + 1) * share] = part.astype(bf16)

    core_rows = 2 * item_ways * chips * item_share
    core_send, core_keep, *results = call(
        other_tiles,
        "other_tiles",
        (shape((core_rows, rank), f32),) * 2
        + tuple(shape((2 * share, rank), bf16) for _ in range(peers))
        + (shape((2 * share, rank), f32),),
        [HBM, HBM, HBM] + [VM] * (8 + 2 * peers),
        (
            *in_hbm(id_args), user_pred, user_imp, own_count, itile, iacc, weights, utile, uacc,
            *(received[k] for k in first_order), *(swapped[k] for k in first_order),
        ),
        (6 * slots * 2 * tile**3, 4000000, 2 * slots * tile * tile),
        id_scratch
        + (
            pltpu.VMEM((peers, 2, shard_rows, rank), bf16),
            pltpu.VMEM((slots, tile, tile), bf16),
            pltpu.VMEM((slots, tile, tile), bf16),
            pltpu.VMEM((2, item_ways * shard_rows, rank), f32),
            pltpu.VMEM((2, user_rows, rank), f32),
        ),
    )
    user_own = results[peers]
    core_recv = core_peer(core_send)
    user_recv = [item_peer(results[k], k + 1) for k in reversed(range(1, peers))]

    chip_rows = 2 * item_ways * item_share

    def fold_core(keep_ref, recv_ref, *outs):
        for k in range(chips):
            rows = pl.ds(k * chip_rows, chip_rows)
            outs[k][...] = (keep_ref[rows] + recv_ref[rows]).astype(outs[k].dtype)

    folded = call(
        fold_core,
        "fold_core",
        (shape((chip_rows, rank), f32),) + tuple(shape((chip_rows, rank), bf16) for _ in range(chips - 1)),
        [VM, VM],
        (core_keep, core_recv),
        (0, 1000, 0),
    )
    middle = chips // 2
    chip_order = [middle, *reversed(range(middle + 1, chips)), *reversed(range(1, middle))]
    chip_recv = [chip_peer(folded[k], k) for k in chip_order]

    def fold_chips(own_ref, *refs):
        recv = refs[: chips - 1]
        outs = refs[chips - 1 :]
        for k in range(item_ways):
            rows = pl.ds(k * 2 * item_share, 2 * item_share)
            part = own_ref[rows]
            for r in recv:
                part = part + r[rows].astype(f32)
            outs[k][...] = part.astype(outs[k].dtype)

    shares = call(
        fold_chips,
        "fold_chips",
        (shape((2 * item_share, rank), f32),) + tuple(shape((2 * item_share, rank), bf16) for _ in range(peers)),
        [VM] * chips,
        (folded[0], *chip_recv),
        (400000000, 1000, 0),
    )
    near_recv = item_peer(results[0], 1)
    item_recv = [item_peer(shares[k], k) for k in reversed(range(1, item_ways))]

    def sum_users(own_ref, *refs):
        part = own_ref[...]
        for r in refs[:-1]:
            part = part + r[...].astype(f32)
        refs[-1][...] = part

    (user_sum,) = call(
        sum_users,
        "sum_users",
        (shape((2 * share, rank), f32),),
        [VM] * peers,
        (user_own, *user_recv),
        (1200000000, 1000, 0),
    )

    def finish(user_ref, item_ref, *refs):
        near, irecv, outs = refs[0], refs[1 : peers + 1], refs[peers + 1 :]
        for m in range(2):
            rows = pl.ds(m * share, share)
            outs[m][...] = user_ref[rows] + near[rows].astype(f32)
            rows = pl.ds(m * item_share, item_share)
            part = item_ref[rows]
            for r in irecv:
                part = part + r[rows].astype(f32)
            outs[2 + m][...] = part

    return call(
        finish,
        "finish",
        (shape((share, rank), f32),) * 2 + (shape((item_share, rank), f32),) * 2,
        [VM] * (3 + peers),
        (user_sum, shares[0], near_recv, *item_recv),
        (0, 1000, 0),
    )


def solution(mesh):
    in_specs = (
        P("user", None),
        P("user", None),
        P("item", None),
        P("item", None),
        P("user", "item", None),
        P("user", "item", None),
        P("user", "item", None),
        P("user", "item", None),
        P("user", "item", None),
        P("user", "item", None, None, None),
        P("user", "item", None, None, None),
    )
    out_specs = (
        P(("user", "item"), None),
        P(("user", "item"), None),
        P(("item", "user"), None),
        P(("item", "user"), None),
    )
    return jax.shard_map(shards, mesh=mesh, in_specs=in_specs, out_specs=out_specs, check_vma=False)
```
